32 devices in a mesh: groups: 2 (over y), ctx: 4 (over z), head: 2 (over x), fsdp: 2 (over core).
Axes of the slice: x: 2, y: 2, z: 4, core: 2. Of those that a mesh axis runs over, the one named last changes fastest.
Arguments:
- queries: float32 [2048, 4096], P(('groups', 'ctx'), ('head', 'fsdp')), parts along dimension 0, may hold values from -6 to 6
- key_input: float32 [2048, 4096], P(('groups', 'ctx'), ('head', 'fsdp')), parts along dimension 0, may hold values from -6 to 6
- value_input: float32 [2048, 4096], P(('groups', 'ctx'), ('head', 'fsdp')), parts along dimension 0, may hold values from -6 to 6
- log_decay: float32 [2048, 4096], P(('groups', 'ctx'), ('head', 'fsdp')), parts along dimension 0, may hold values from -1 to 0
- write_rate: float32 [2048, 32], P(('groups', 'ctx'), ('head', 'fsdp')), parts along dimension 0, may hold values from 0.02 to 0.2
- start_state: float32 [64, 128, 128], P(('groups', 'head', 'fsdp')), parts along dimension 0, may hold values from -4 to 4
- out_grad: float32 [2048, 4096], P(('groups', 'ctx'), ('head', 'fsdp')), parts along dimension 0, may hold values from -6 to 6
- end_grad: float32 [64, 128, 128], P(('groups', 'head', 'fsdp')), parts along dimension 0, may hold values from -4 to 4
- moe_input: bfloat16 [2048, 1152], P(('groups', 'ctx', 'fsdp')), parts along dimension 0, may hold values from -6 to 6
- moe_grad: float32 [2048, 1152], P(('groups', 'ctx', 'fsdp')), parts along dimension 0, may hold values from -6 to 6
- expert_ids: int32 [2048, 8], P(('groups', 'ctx', 'fsdp')), parts along dimension 0, may hold values from 0 to 31, all different within a row; in each aligned block of 128 rows (0 to 127, 128 to 255, ...) at most 48 rows name the same one
- gate_weights: float32 [2048, 8], P(('groups', 'ctx', 'fsdp')), parts along dimension 0, may hold values from 0.05 to 0.25
- gate_matrix: bfloat16 [32, 1152, 1024], P('ctx', 'fsdp', 'head'), may hold values from -0.1875 to 0.1875
- up_matrix: bfloat16 [32, 1152, 1024], P('ctx', 'fsdp', 'head'), may hold values from -0.1875 to 0.1875
- down_matrix: bfloat16 [32, 1024, 1152], P('ctx', 'head', 'fsdp'), may hold values from -0.1875 to 0.1875
Outputs:
- query_grad: float32 [2048, 4096], P(('groups', 'ctx'), ('head', 'fsdp')), parts along dimension 0
- key_grad: float32 [2048, 4096], P(('groups', 'ctx'), ('head', 'fsdp')), parts along dimension 0
- value_grad: float32 [2048, 4096], P(('groups', 'ctx'), ('head', 'fsdp')), parts along dimension 0
- decay_grad: float32 [2048, 4096], P(('groups', 'ctx'), ('head', 'fsdp')), parts along dimension 0
- rate_grad: float32 [2048, 32], P(('groups', 'ctx'), ('head', 'fsdp')), parts along dimension 0
- state_grads: float32 [8, 32, 128, 128], P(('groups', 'ctx'), ('head', 'fsdp')), parts along dimension 0
- input_grads: float32 [2048, 1152], P(('groups', 'ctx', 'fsdp'), 'head'), parts along dimension 0
- gate_grads: float32 [2048, 8], P(('groups', 'ctx', 'fsdp'), 'head'), parts along dimension 0
The draws below stay inside these ranges and needn't reach their ends.
There are 2 independent parts, one for each index of `groups`. The reference program is written for one: setup_inputs(seed, part) draws one part's arguments, and reference() takes and returns one part's arrays. A program takes and returns all parts, laid end to end along the dimension named above; an argument that names none is the same for every part. Nothing has to cross between parts.
Inputs may be any that keep to these rules, and one draw needn't show every extreme that they name: `expert_ids`: each row names 8 different experts; within the 128 rows of one device no expert is named more than 48 times, a bound that some block reaches.
All inputs are finite; a program needn't handle non-finite values.
Results may differ from the reference program's by a relative error of at most 0.014.
Values may be sent and summed in bfloat16 or wider, within the bound.
No kernel may reach another device: no remote copies, remote signals or barrier semaphores. Data moves between devices by JAX's collectives and lax.ppermute only.
A program may use at most 192 MiB of HBM per device.

```python
import math
import jax
import jax.numpy as jnp
import numpy as np
from jax import lax

D = 1152
HEADS = 32
K = 128
V = 128
FF = 1024
TOPK = 8
EXPERTS = 32
T_DEV = 256
WINDOW_TOKENS = 1024
MOE_ROWS = 128
CAP = 48
N_CTX = 4
N_HEAD = 2


def draw_log_decay(key, part):
    key = jax.random.fold_in(key, 7)
    key_sequence = jax.random.split(key, 7)
    channels = HEADS * K
    fast_share = 0.5
    fast_mask = (jax.random.uniform(key_sequence[0], (channels,)) < fast_share).astype(jnp.float32)
    slow_rate = math.log(10.0) / WINDOW_TOKENS * jnp.exp(jax.random.uniform(key_sequence[1], (channels,), minval=math.log(0.1), maxval=math.log(0.5)))
    fast_rate = jnp.exp(jax.random.uniform(key_sequence[2], (channels,), minval=math.log(1.0 / 50.0), maxval=math.log(1.0 / 30.0)))
    baseline_rate = fast_mask * fast_rate + (1.0 - fast_mask) * slow_rate
    jaggedness = jax.random.uniform(key_sequence[3], (WINDOW_TOKENS, channels), minval=0.5, maxval=1.5)
    scale_per_block = jnp.exp(jax.random.uniform(key_sequence[4], (WINDOW_TOKENS // T_DEV, 1, channels), minval=math.log(0.6), maxval=math.log(1.6)))
    scale_per_block = jnp.broadcast_to(scale_per_block, (WINDOW_TOKENS // T_DEV, T_DEV, channels)).reshape(WINDOW_TOKENS, channels)
    spike_rows = jax.random.randint(key_sequence[5], (3,), 0, WINDOW_TOKENS)
    spike_mask = jnp.any(jnp.arange(WINDOW_TOKENS)[:, None] == spike_rows[None, :], axis=1).astype(jnp.float32)
    loss_fraction = jax.random.uniform(key_sequence[6], (WINDOW_TOKENS, 1), minval=0.2, maxval=0.5)
    spike_events = spike_mask[:, None] * jnp.log(1.0 - loss_fraction)
    return (spike_events - baseline_rate[None, :] * jaggedness * scale_per_block).astype(jnp.float32)


def steps_of(stream_key, extent, shards, smallest, top_value):
    gain = 1.0
    for axis_at, blocks in shards:
        heights = jax.random.uniform(jax.random.fold_in(jax.random.fold_in(stream_key, 6), axis_at), (blocks,), jnp.float32, smallest / len(shards), top_value / len(shards))
        gain = gain * jnp.repeat(jnp.exp(heights), extent[axis_at] // blocks).reshape((-1,) + (1,) * (len(extent) - 1 - axis_at))
    return gain


def deal_out(key, own, number, rows, amount, top, bound, lean):
    order = jax.random.permutation(key, amount)
    heavy_load, common = load_shares(amount, rows * top, bound, lean, True), load_shares(amount, rows * top, bound, lean, False)
    places = jnp.arange(amount)

    def named(tallies, turn):
        used = int((tallies > 0).sum())
        fixed = max(1, used // 4)
        moved = fixed + (places - fixed + turn * (used - fixed)) % max(1, amount - fixed)
        return jnp.zeros((amount,), jnp.int32).at[order[jnp.where(places < fixed, places, moved)]].set(jnp.asarray(tallies, jnp.int32))

    tallies = jnp.where(number % 4 == 0, named(heavy_load, number // 4), named(common, number - number // 4 - 1))
    mixed = jax.random.permutation(jax.random.fold_in(own, 3), amount)
    donor, sink = mixed[0:amount // 2 * 2:2], mixed[1:amount // 2 * 2:2]
    margin = jnp.minimum(tallies[donor] - 1, bound - tallies[sink]) // 2
    margin = jnp.where((donor == order[0]) | (sink == order[0]) | (tallies[sink] == 0), 0, jnp.maximum(margin, 0))
    moved = jax.random.randint(jax.random.fold_in(own, 4), (amount // 2,), 0, 1 << 20) % (margin + 1)
    tallies = tallies.at[donor].add(-moved).at[sink].add(moved)
    items = jnp.searchsorted(jnp.cumsum(tallies), jnp.arange(rows * top), side="right").astype(jnp.int32)
    listing = items.reshape(top, rows).T
    listing = listing[jax.random.permutation(jax.random.fold_in(own, 1), rows)]
    turn = jax.random.randint(jax.random.fold_in(own, 2), (rows, 1), 0, top)
    return jnp.take_along_axis(listing, (jnp.arange(top)[None, :] + turn) % top, axis=1)


def load_shares(count, total, bound, skew, full):
    loads = [(1 << 20) // math.isqrt(grade ** skew) + 1 for grade in range(1, count + 1)]
    largest = bound if full else min(bound, max(-(-total // count), total * loads[0] // sum(loads)))
    least = 1 if total - largest >= count - 1 else 0
    counts, spare = [largest] + [least] * (count - 1), total - largest - least * (count - 1)
    while spare > 0:
        free = [i for i in range(1, count) if counts[i] < largest] or [i for i in range(1, count) if counts[i] < bound]
        whole, budget = sum([loads[i] for i in free]), spare
        for i in free:
            extra = min(bound - counts[i], max(1, budget * loads[i] // whole), spare)
            counts[i] = counts[i] + extra
            spare = spare - extra
    return np.array(counts)


def noise(stream_key, dims, deviation, limit, cuts=(), kind=jnp.bfloat16):
    array = deviation * jax.random.normal(stream_key, dims, jnp.float32)
    if cuts:
        array = array * steps_of(stream_key, dims, cuts, -0.22, 0.18)
    return jnp.clip(array, -limit, limit).astype(kind)


def setup_inputs(seed: int = 0, part: int = 0) -> dict:
    seeds = jax.random.split(jax.random.key(seed), 16)
    part_keys = jax.random.split(jax.random.fold_in(seeds[15], part), 16)
    queries = noise(part_keys[0], (WINDOW_TOKENS, HEADS * K), 1.0, 6.0, ((0, 4), (1, 4)), jnp.float32)
    key_input = noise(part_keys[1], (WINDOW_TOKENS, HEADS * K), 1.0, 6.0, ((0, 4), (1, 4)), jnp.float32)
    value_input = noise(part_keys[2], (WINDOW_TOKENS, HEADS * V), 1.0, 6.0, ((0, 4), (1, 4)), jnp.float32)
    log_decay = draw_log_decay(jax.random.fold_in(jax.random.fold_in(seeds[15], part), 71), part)
    write_rate = jnp.clip(jnp.exp(math.log(0.2) - 2.3025851 * jax.random.uniform(part_keys[4], (WINDOW_TOKENS, HEADS), jnp.float32) ** steps_of(part_keys[4], (WINDOW_TOKENS, HEADS), ((0, 4), (1, 4)), -0.2, 0.2)), 0.02, 0.2)
    start_state = noise(part_keys[5], (HEADS, K, V), 0.5, 4.0, ((0, 4),), jnp.float32)
    out_grad = noise(part_keys[6], (WINDOW_TOKENS, HEADS * V), 1.0, 6.0, ((0, 4), (1, 4)), jnp.float32)
    end_grad = noise(part_keys[7], (HEADS, K, V), 0.5, 4.0, ((0, 4),), jnp.float32)
    moe_input = noise(part_keys[8], (WINDOW_TOKENS, D), 1.0, 6.0, ((0, 8),))
    moe_grad = noise(part_keys[9], (WINDOW_TOKENS, D), 1.0, 6.0, ((0, 8),), jnp.float32)
    expert_ids_keys = jax.random.split(jax.random.fold_in(part_keys[10], 1), WINDOW_TOKENS // MOE_ROWS)
    expert_ids_turns = jax.random.permutation(jax.random.fold_in(part_keys[10], 3), WINDOW_TOKENS // MOE_ROWS)
    expert_ids = jax.vmap(lambda own, number: deal_out(jax.random.fold_in(part_keys[10], 2), own, number, MOE_ROWS, EXPERTS, TOPK, CAP, 2))(expert_ids_keys, expert_ids_turns).reshape((WINDOW_TOKENS, TOPK))
    gate_weights = jnp.clip(0.05 + 0.2 * jax.random.uniform(part_keys[11], (WINDOW_TOKENS, TOPK), jnp.float32) ** steps_of(part_keys[11], (WINDOW_TOKENS, TOPK), ((0, 8),), -0.2, 0.2), 0.05, 0.25)
    gate_matrix = noise(seeds[12], (EXPERTS, D, FF), D ** -0.5, 0.1875, ((0, 4), (1, 2), (2, 2)))
    up_matrix = noise(seeds[13], (EXPERTS, D, FF), D ** -0.5, 0.1875, ((0, 4), (1, 2), (2, 2)))
    down_matrix = noise(seeds[14], (EXPERTS, FF, D), FF ** -0.5, 0.1875, ((0, 4), (1, 2), (2, 2)))
    return {"queries": queries, "key_input": key_input, "value_input": value_input, "log_decay": log_decay, "write_rate": write_rate, "start_state": start_state, "out_grad": out_grad, "end_grad": end_grad, "moe_input": moe_input, "moe_grad": moe_grad, "expert_ids": expert_ids, "gate_weights": gate_weights, "gate_matrix": gate_matrix, "up_matrix": up_matrix, "down_matrix": down_matrix}


HIGHEST = lax.Precision.HIGHEST

def unit_rows(matrix):
    return matrix * lax.rsqrt(lax.optimization_barrier(jnp.sum(matrix * matrix, axis=-1, keepdims=True)) + 1e-06)

def recurrence(memory_in, unit_query, unit_key, written, decays, write_rates):

    def advance(memory, inputs):
        query_t, key_t, write_t, decay_t, rate_t = inputs
        memory = jnp.exp(decay_t)[:, :, None] * memory
        recalled = jnp.einsum('hk,hkw->hw', key_t, memory, precision=HIGHEST)
        memory = memory + (rate_t[:, None] * key_t)[:, :, None] * (write_t - recalled)[:, None, :]
        output_t = jnp.einsum('hk,hkw->hw', query_t, memory, precision=HIGHEST)
        return (memory, output_t)
    return lax.scan(advance, memory_in, (unit_query, unit_key, written, decays, write_rates))

def head_gradients(inputs):
    query_h, key_h, value_h, decay_h, rate_h, start_h, outgrad_h, endgrad_h = inputs

    def total_loss(start, nudges, query_in, key_in, value_in, decay_in, rate_in):
        split = (N_CTX, T_DEV, 1, -1)

        def one_section(memory, pieces):
            nudge, query_s, key_s, value_s, decay_s, rate_s = pieces
            memory = memory + nudge[None]
            memory, outputs = recurrence(memory, unit_rows(query_s), unit_rows(key_s), value_s, decay_s, rate_s)
            return (memory, outputs)
        last_memory, outputs = lax.scan(one_section, start[None], (nudges, query_in.reshape(split), key_in.reshape(split), value_in.reshape(split), decay_in.reshape(split), rate_in.reshape(N_CTX, T_DEV, 1)))
        return jnp.sum(outputs.reshape(WINDOW_TOKENS, -1) * outgrad_h) + jnp.sum(last_memory[0] * endgrad_h)
    nudges = jnp.zeros((N_CTX,) + start_h.shape, jnp.float32)
    return jax.grad(total_loss, argnums=(1, 2, 3, 4, 5, 6))(start_h, nudges, query_h, key_h, value_h, decay_h, rate_h)

def per_head(matrix):
    return matrix.reshape(WINDOW_TOKENS, HEADS, -1).transpose(1, 0, 2)

def per_token(matrix):
    return matrix.transpose(1, 0, 2).reshape(WINDOW_TOKENS, -1)

def reference(queries, key_input, value_input, log_decay, write_rate, start_state, out_grad, end_grad, moe_input, moe_grad, expert_ids, gate_weights, gate_matrix, up_matrix, down_matrix):
    stacked = (per_head(queries), per_head(key_input), per_head(value_input), per_head(log_decay), write_rate.T, start_state, per_head(out_grad), end_grad)
    nudge_grad, query_g, key_g, value_g, decay_g, rate_g = lax.map(head_gradients, stacked)
    state_grads = nudge_grad.transpose(1, 0, 2, 3)
    blocks = WINDOW_TOKENS // MOE_ROWS
    flat_ids = expert_ids.reshape(blocks, MOE_ROWS * TOPK)
    chosen = (flat_ids[..., None] == jnp.arange(EXPERTS, dtype=jnp.int32)).astype(jnp.int32)
    ranks = lax.optimization_barrier(jnp.sum((jnp.cumsum(chosen, axis=1) - chosen) * chosen, axis=-1))
    slot_place = jnp.arange(blocks, dtype=jnp.int32)[:, None] * CAP + ranks
    assigned = jnp.arange(WINDOW_TOKENS * TOPK, dtype=jnp.int32).reshape(blocks, -1)
    slot_table = jnp.full((EXPERTS, blocks * CAP), WINDOW_TOKENS * TOPK, jnp.int32)
    slot_table = slot_table.at[flat_ids.reshape(-1), slot_place.reshape(-1)].set(assigned.reshape(-1))
    rows_pad = jnp.concatenate([moe_input, jnp.zeros((1, D), jnp.bfloat16)], axis=0)
    grads_pad = jnp.concatenate([moe_grad.astype(jnp.bfloat16), jnp.zeros((1, D), jnp.bfloat16)], axis=0)
    weight_pad = jnp.concatenate([gate_weights.reshape(-1), jnp.zeros((1,), jnp.float32)], axis=0)

    def expert_terms(inputs):
        table_e, gate_e, up_e, down_e = inputs
        token_of = table_e // TOPK
        row_values = rows_pad[token_of]
        grad_values = grads_pad[token_of]
        slot_weight = weight_pad[table_e]
        gate_pre = jnp.dot(row_values, gate_e, preferred_element_type=jnp.float32)
        up_pre = jnp.dot(row_values, up_e, preferred_element_type=jnp.float32)
        raw_grad = jnp.dot(grad_values, down_e.T, preferred_element_type=jnp.float32)
        sigmoid_gate = jax.nn.sigmoid(gate_pre)
        activated = gate_pre * sigmoid_gate
        hidden = (activated * up_pre).astype(jnp.bfloat16)
        gate_part = lax.optimization_barrier(jnp.sum(hidden.astype(jnp.float32) * raw_grad, axis=-1))
        scaled = raw_grad * slot_weight[:, None]
        gate_back = (scaled * up_pre * sigmoid_gate * (1.0 + gate_pre * (1.0 - sigmoid_gate))).astype(jnp.bfloat16)
        up_back = (scaled * activated).astype(jnp.bfloat16)
        slot_count = gate_back.shape[0]
        pieces = jnp.einsum('sgf,dgf->sgd', gate_back.astype(jnp.float32).reshape(slot_count, N_HEAD, -1), gate_e.astype(jnp.float32).reshape(D, N_HEAD, -1), precision=HIGHEST)
        pieces = pieces + jnp.einsum('sgf,dgf->sgd', up_back.astype(jnp.float32).reshape(slot_count, N_HEAD, -1), up_e.astype(jnp.float32).reshape(D, N_HEAD, -1), precision=HIGHEST)
        rounded = lax.optimization_barrier(pieces.astype(jnp.bfloat16)).astype(jnp.float32)
        return (lax.optimization_barrier(jnp.sum(rounded, axis=1)), gate_part)
    slot_terms, slot_gates = lax.map(expert_terms, (slot_table, gate_matrix, up_matrix, down_matrix))
    input_grads = jnp.zeros((WINDOW_TOKENS + 1, D), jnp.float32).at[(slot_table // TOPK).reshape(-1)].add(slot_terms.reshape(-1, D))[:WINDOW_TOKENS]
    gate_grads = jnp.zeros((WINDOW_TOKENS * TOPK + 1,), jnp.float32).at[slot_table.reshape(-1)].add(slot_gates.reshape(-1))[:-1].reshape(WINDOW_TOKENS, TOPK)
    return (per_token(query_g), per_token(key_g), per_token(value_g), per_token(decay_g), rate_g.T, state_grads, input_grads, gate_grads)
```

```python
import functools

import jax
import jax.numpy as jnp
from jax import lax
from jax.experimental import pallas as pl
from jax.experimental.pallas import tpu as pltpu
from jax.sharding import PartitionSpec as P

BF = jnp.bfloat16
F32 = jnp.float32
VMEM_BYTES = 48 * 1024 * 1024


def dot(a, b):
    return lax.dot_general(
        a.astype(BF), b.astype(BF), (((1,), (0,)), ((), ())), preferred_element_type=F32
    )


def dot_t(a, b):
    return lax.dot_general(
        a.astype(BF), b.astype(BF), (((1,), (1,)), ((), ())), preferred_element_type=F32
    )


def tdot(a, b):
    return lax.dot_general(
        a.astype(BF), b.astype(BF), (((0,), (0,)), ((), ())), preferred_element_type=F32
    )


def halves(x, axis):
    high = x.astype(BF)
    return jnp.concatenate([high, (x - high.astype(F32)).astype(BF)], axis=axis)


def places(size, axis):
    return lax.broadcasted_iota(jnp.int32, (size, size), axis)


def column(matrix, at):
    lanes = lax.broadcasted_iota(jnp.int32, matrix.shape, 1)
    return jnp.sum(jnp.where(lanes == at, matrix, 0.0), axis=1, keepdims=True)


def to_column(row):
    size = row.shape[1]
    spread = jnp.broadcast_to(row, (size, size))
    return jnp.sum(jnp.where(places(size, 0) == places(size, 1), spread, 0.0), axis=1, keepdims=True)


def inverse_less_one(scores):
    size = scores[0].shape[0]
    rows, cols = places(size, 0), places(size, 1)
    eye = (rows == cols).astype(F32)
    span, off = 1, None
    while span < size:
        joins = (rows // (2 * span) == cols // (2 * span)) & (rows // span != cols // span)
        parts = [jnp.where(joins, a, 0.0).astype(BF) for a in scores]
        if off is None:
            off = [-p.astype(F32) for p in parts]
        else:
            full = [(o + eye).astype(BF) for o in off]
            half = [dot(p, f) for p, f in zip(parts, full)]
            off = [o - dot(f, h) for o, f, h in zip(off, full, half)]
        span *= 2
    return off


def maps_kernel(
    chunk,
    width,
    heads_step,
    query_ref,
    key_ref,
    value_ref,
    decay_ref,
    rate_ref,
    grad_ref,
    transfer_ref,
    carried_ref,
    own_ref,
    cum_ref,
    query_l_ref,
    key_l_ref,
    back_ref,
    lower_ref,
    score_ref,
):
    tokens = query_ref.shape[0]
    chunks = tokens // chunk
    rows, cols = places(chunk, 0), places(chunk, 1)
    tri = (rows >= cols).astype(BF)
    tri = jnp.concatenate([tri, tri], axis=1)
    units = [(h, i) for h in range(heads_step) for i in range(chunks)]
    first = pl.program_id(0) * heads_step
    rates = [column(rate_ref[...], first + h) for h in range(heads_step)]

    def part(ref, unit):
        h, i = unit
        return ref[i * chunk : (i + 1) * chunk, h * width : (h + 1) * width]

    def unit_rows(x):
        return x * lax.rsqrt(jnp.sum(x * x, axis=-1, keepdims=True) + 1e-06)

    cums = [dot(tri, halves(part(decay_ref, u), 0)) for u in units]
    queries = [unit_rows(part(query_ref, u)) for u in units]
    keys = [unit_rows(part(key_ref, u)) for u in units]
    values = [part(value_ref, u) for u in units]
    middles = [0.5 * c[chunk - 1 : chunk, :] for c in cums]
    lifts = [jnp.exp(c - m) for c, m in zip(cums, middles)]
    sinks = [jnp.exp(m - c) for c, m in zip(cums, middles)]
    key_l = [(k * e).astype(BF) for k, e in zip(keys, lifts)]
    query_l = [(q * e).astype(BF) for q, e in zip(queries, lifts)]
    back = [
        (k * e * rates[h][i * chunk : (i + 1) * chunk]).astype(BF)
        for k, e, (h, i) in zip(keys, sinks, units)
    ]
    both = [dot_t(jnp.concatenate([k, q], axis=0), b) for k, q, b in zip(key_l, query_l, back)]
    key_scores = [jnp.where(rows > cols, s[:chunk], 0.0) for s in both]
    scores = [jnp.where(rows >= cols, s[chunk:], 0.0).astype(BF) for s in both]
    lower = [o.astype(BF) for o in inverse_less_one(key_scores)]
    wide = [jnp.concatenate([k, v.astype(BF)], axis=1) for k, v in zip(key_l, values)]
    solved = [
        dot(o, w) + jnp.concatenate([k.astype(F32), v], axis=1)
        for o, w, k, v in zip(lower, wide, key_l, values)
    ]
    solved = [s.astype(BF) for s in solved]
    stepped = [tdot(b, s) for b, s in zip(back, solved)]
    reads = [q.astype(F32) - dot(p, s[:, :width]) for q, p, s in zip(query_l, scores, solved)]
    mids = [to_column(jnp.exp(m)) for m in middles]
    owns = [m * tdot(r, part(grad_ref, u)) for m, r, u in zip(mids, reads, units)]
    for n, u in enumerate(units):
        h, i = u
        span = slice(i * chunk, (i + 1) * chunk)
        lanes = slice(h * width, (h + 1) * width)
        cum_ref[span, lanes] = cums[n]
        query_l_ref[span, lanes] = query_l[n]
        key_l_ref[span, lanes] = key_l[n]
        back_ref[span, lanes] = back[n]
        lower_ref[h, span, :] = lower[n]
        score_ref[h, span, :] = scores[n]
    eye = (places(width, 0) == places(width, 1)).astype(F32)
    for h in range(heads_step):
        state = None
        for i in range(chunks):
            n = h * chunks + i
            mid, step = mids[n], stepped[n][:, :width]
            entering = jnp.concatenate([eye, jnp.zeros_like(eye)], axis=1) if i == 0 else state
            scaled = mid * entering
            moved = scaled - dot(step, scaled)
            carried = jnp.concatenate([jnp.zeros_like(eye), stepped[n][:, width:]], axis=1)
            state = mid * (moved + carried)
        transfer_ref[h] = state[:, :width]
        carried_ref[h] = state[:, width:]
        total = owns[h * chunks + chunks - 1]
        for i in range(chunks - 2, -1, -1):
            n = h * chunks + i
            scaled = mids[n] * total
            total = owns[n] + mids[n] * (scaled - tdot(stepped[n][:, :width], scaled))
        own_ref[h] = total


def grads_kernel(
    chunk,
    width,
    heads_step,
    query_ref,
    key_ref,
    value_ref,
    rate_ref,
    grad_ref,
    cum_ref,
    query_l_ref,
    key_l_ref,
    back_ref,
    lower_ref,
    score_ref,
    entry_ref,
    exit_ref,
    query_grad_ref,
    key_grad_ref,
    value_grad_ref,
    decay_grad_ref,
    rate_grad_ref,
    state_grad_ref,
):
    tokens = query_ref.shape[0]
    chunks = tokens // chunk
    rows, cols = places(chunk, 0), places(chunk, 1)
    tri = (rows <= cols).astype(BF)
    tri = jnp.concatenate([tri, tri], axis=1)
    first = pl.program_id(0) * heads_step
    heads = range(heads_step)
    rates = [column(rate_ref[...], first + h) for h in heads]

    def part(ref, h, i):
        return ref[i * chunk : (i + 1) * chunk, h * width : (h + 1) * width]

    def mat(ref, h, i):
        return ref[h, i * chunk : (i + 1) * chunk, :]

    cums = {(h, i): part(cum_ref, h, i) for i in range(chunks) for h in heads}
    middles = {u: 0.5 * c[chunk - 1 : chunk, :] for u, c in cums.items()}
    mids = {u: to_column(jnp.exp(m)) for u, m in middles.items()}
    states = {(h, 0): entry_ref[h] for h in heads}
    scaled, updates = {}, {}
    for i in range(chunks):
        for h in heads:
            u = (h, i)
            scaled[u] = mids[u] * states[u]
        rests = [part(value_ref, h, i) - dot(part(key_l_ref, h, i), scaled[h, i]) for h in heads]
        for h in heads:
            updates[h, i] = (rests[h] + dot(mat(lower_ref, h, i), rests[h])).astype(BF)
        for h in heads:
            moved = scaled[h, i] + tdot(part(back_ref, h, i), updates[h, i])
            states[h, i + 1] = mids[h, i] * moved
    out = {(h, chunks): exit_ref[h] for h in heads}
    rest_grads, lifted, out_grads = {}, {}, {}
    for i in range(chunks - 1, -1, -1):
        update_grads = []
        for h in heads:
            lifted[h, i] = mids[h, i] * out[h, i + 1]
            out_grads[h, i] = part(grad_ref, h, i).astype(BF)
            got = tdot(mat(score_ref, h, i), out_grads[h, i])
            update_grads.append(got + dot(part(back_ref, h, i), lifted[h, i]))
        for h in heads:
            rest = update_grads[h] + tdot(mat(lower_ref, h, i), update_grads[h])
            value_grad_ref[i * chunk : (i + 1) * chunk, h * width : (h + 1) * width] = rest
            rest_grads[h, i] = rest.astype(BF)
        for h in heads:
            left = jnp.concatenate([part(query_l_ref, h, i), part(key_l_ref, h, i)], axis=0)
            right = jnp.concatenate([out_grads[h, i], -rest_grads[h, i]], axis=0)
            out[h, i] = mids[h, i] * (lifted[h, i] + tdot(left, right))
    for h in heads:
        state_grad_ref[h] = out[h, 0]
    units = [(h, i) for i in range(chunks) for h in heads]
    joint = [jnp.concatenate([-rest_grads[u], out_grads[u]], axis=0) for u in units]
    pairs = [dot_t(j, updates[u]) for j, u in zip(joint, units)]
    key_pairs = [jnp.where(rows > cols, p[:chunk], 0.0).astype(BF) for p in pairs]
    query_pairs = [jnp.where(rows >= cols, p[chunk:], 0.0).astype(BF) for p in pairs]
    pairs = [jnp.concatenate([k, q], axis=0) for k, q in zip(key_pairs, query_pairs)]
    left_grads = [
        dot(p, part(back_ref, *u)) + dot_t(j, scaled[u]) for p, j, u in zip(pairs, joint, units)
    ]
    back_grads = [
        tdot(p, jnp.concatenate([part(key_l_ref, *u), part(query_l_ref, *u)], axis=0))
        + dot_t(updates[u], lifted[u])
        for p, u in zip(pairs, units)
    ]
    ones = jnp.ones((8, 2 * width), BF)
    crossing = [
        dot_t(ones, halves(out[h, i + 1] * states[h, i + 1], 1))[:1] for h, i in units
    ]
    slopes = [
        part(key_l_ref, *u).astype(F32) * l[:chunk]
        + part(query_l_ref, *u).astype(F32) * l[chunk:]
        - part(back_ref, *u).astype(F32) * b
        for u, l, b in zip(units, left_grads, back_grads)
    ]
    decays = [dot(tri, halves(s, 0)) + c for s, c in zip(slopes, crossing)]
    if heads_step * pl.num_programs(0) == rate_grad_ref.shape[1]:
        lanes = lax.broadcasted_iota(jnp.int32, (chunk, rate_grad_ref.shape[1]), 1)
    for n, (h, i) in enumerate(units):
        span = slice(i * chunk, (i + 1) * chunk)
        at = slice(h * width, (h + 1) * width)
        decay_grad_ref[span, at] = decays[n]
        gap = cums[h, i] - middles[h, i]
        lift, sink = jnp.exp(gap), jnp.exp(-gap)
        rate = rates[h][span]
        query, key = query_ref[span, at], key_ref[span, at]
        query_norm = lax.rsqrt(jnp.sum(query * query, axis=-1, keepdims=True) + 1e-06)
        key_norm = lax.rsqrt(jnp.sum(key * key, axis=-1, keepdims=True) + 1e-06)
        query, key = query * query_norm, key * key_norm
        query_grad = left_grads[n][chunk:] * lift
        sunk = back_grads[n] * sink
        key_grad = left_grads[n][:chunk] * lift + rate * sunk
        rate_grad = jnp.sum(sunk * key, axis=-1, keepdims=True)
        query_grad_ref[span, at] = query_norm * (
            query_grad - query * jnp.sum(query * query_grad, axis=-1, keepdims=True)
        )
        key_grad_ref[span, at] = key_norm * (
            key_grad - key * jnp.sum(key * key_grad, axis=-1, keepdims=True)
        )
        rate_grad_ref[span, :] = jnp.where(lanes == first + h, rate_grad, rate_grad_ref[span, :])


def specs_of(tokens, width, chunk, heads_step, rate_heads):
    lanes = pl.BlockSpec((tokens, heads_step * width), lambda h: (0, h))
    rate = pl.BlockSpec((tokens, rate_heads), lambda h: (0, 0))
    square = pl.BlockSpec((heads_step, tokens, chunk), lambda h: (h, 0, 0))
    state = pl.BlockSpec((heads_step, width, width), lambda h: (h, 0, 0))
    return lanes, rate, square, state


def section_maps(queries, key_input, value_input, log_decay, write_rate, out_grad):
    tokens, heads = write_rate.shape
    width = queries.shape[1] // heads
    chunk = min(128, tokens)
    heads_step = 2 if heads % 2 == 0 else 1
    lanes, rate, square, state = specs_of(tokens, width, chunk, heads_step, heads)
    shape = jax.ShapeDtypeStruct
    return pl.pallas_call(
        functools.partial(maps_kernel, chunk, width, heads_step),
        grid=(heads // heads_step,),
        in_specs=[lanes, lanes, lanes, lanes, rate, lanes],
        out_specs=[state, state, state, lanes, lanes, lanes, lanes, square, square],
        out_shape=[shape((heads, width, width), F32)] * 3
        + [shape(queries.shape, F32)]
        + [shape(queries.shape, BF)] * 3
        + [shape((heads, tokens, chunk), BF)] * 2,
        compiler_params=pltpu.CompilerParams(vmem_limit_bytes=VMEM_BYTES),
        name="section_maps",
    )(queries, key_input, value_input, log_decay, write_rate, out_grad)


def section_grads(
    queries, key_input, value_input, write_rate, out_grad, saved, entry_state, exit_grad
):
    tokens, heads = write_rate.shape
    width = queries.shape[1] // heads
    chunk = min(128, tokens)
    heads_step = 2 if heads % 2 == 0 else 1
    lanes, rate, square, state = specs_of(tokens, width, chunk, heads_step, heads)
    shape = jax.ShapeDtypeStruct
    return pl.pallas_call(
        functools.partial(grads_kernel, chunk, width, heads_step),
        grid=(heads // heads_step,),
        in_specs=[lanes, lanes, lanes, rate, lanes]
        + [lanes] * 4
        + [square] * 2
        + [state] * 2,
        out_specs=[lanes, lanes, lanes, lanes, rate, state],
        out_shape=[shape(queries.shape, F32)] * 4
        + [shape((tokens, heads), F32), shape((heads, width, width), F32)],
        compiler_params=pltpu.CompilerParams(vmem_limit_bytes=VMEM_BYTES),
        name="section_grads",
    )(queries, key_input, value_input, write_rate, out_grad, *saved, entry_state, exit_grad)


def experts_kernel(
    capacity,
    part_width,
    sources,
    place_ref,
    *refs,
):
    row_refs, grad_refs = refs[:sources], refs[sources : 2 * sources]
    rest = refs[2 * sources :]
    gate_own, gate_far, up_own, up_far, down_own, down_far, out_own, out_far = rest[:8]
    gate_s, up_s, down_s, rows_s, grads_s, pieces_s, ranks_s, weights_s = rest[8:]
    step, steps = pl.program_id(0), pl.num_programs(0)
    mine = place_ref[0]
    head_at = place_ref[1]
    first = place_ref[2]
    tokens = row_refs[0].shape[0]
    parts, padded, hidden_width = gate_s.shape
    experts = ranks_s.shape[1]
    many = rows_s.shape[0]

    def choice(source, at):
        rank = ranks_s[source, pl.ds(at, 1), :]
        slot = lax.broadcasted_iota(jnp.int32, (capacity, tokens), 0).astype(F32)
        return slot == rank

    @pl.when(step == 0)
    def dispatch():
        gate_s[...] = jnp.zeros_like(gate_s)
        up_s[...] = jnp.zeros_like(up_s)
        down_s[...] = jnp.zeros_like(down_s)
        before = (places(tokens, 0) < places(tokens, 1)).astype(BF)
        for s in range(sources):
            start = part_width // 128 * 128
            tile = row_refs[s][:, start : start + 128].astype(F32)
            offset = part_width - start
            dense = jnp.transpose(tile)[offset : offset + experts]
            named = dense > 0.0
            rank = dot(named.astype(F32), before)
            ranks_s[s] = jnp.where(named, rank, -1.0)
            weights_s[s] = dense
            picks = [choice(s, first + e).astype(F32).astype(BF) for e in range(many)]
            pick = jnp.concatenate(picks, axis=0)
            rows = dot(pick, row_refs[s][...]).astype(BF)
            grads = dot(pick, grad_refs[s][...]).astype(BF)
            for e in range(many):
                rows_s[e, s * capacity : (s + 1) * capacity] = rows[e * capacity : (e + 1) * capacity]
                grads_s[e, s * capacity : (s + 1) * capacity] = grads[e * capacity : (e + 1) * capacity]

    for ref, own, far in ((gate_s, gate_own, gate_far), (up_s, up_own, up_far)):
        ref[mine, :part_width, :] = own[0]
        ref[1 - mine, :part_width, :] = far[0]
    down_s[mine, :, :part_width] = down_own[0]
    down_s[1 - mine, :, :part_width] = down_far[0]
    at = first + step
    gate_pre = up_pre = raw_grad = 0.0
    for p in range(parts):
        rows = rows_s[step, :, p * padded : (p + 1) * padded]
        grads = grads_s[step, :, p * padded : (p + 1) * padded]
        gate_pre = gate_pre + dot(rows, gate_s[p])
        up_pre = up_pre + dot(rows, up_s[p])
        raw_grad = raw_grad + dot_t(grads, down_s[p])
    weight = jnp.concatenate(
        [
            jnp.sum(
                jnp.where(choice(s, at), weights_s[s, pl.ds(at, 1), :], 0.0), axis=1, keepdims=True
            )
            for s in range(sources)
        ],
        axis=0,
    )
    sigmoid = jax.nn.sigmoid(gate_pre)
    activated = gate_pre * sigmoid
    hidden = (activated * up_pre).astype(BF).astype(F32)
    gate_part = jnp.sum(hidden * raw_grad, axis=1, keepdims=True)
    scaled = raw_grad * weight
    gate_back = (scaled * up_pre * sigmoid * (1.0 + gate_pre * (1.0 - sigmoid))).astype(BF)
    up_back = (scaled * activated).astype(BF)
    lanes = lax.broadcasted_iota(jnp.int32, (1, padded), 1)
    for p in range(parts):
        piece = dot_t(gate_back, gate_s[p]) + dot_t(up_back, up_s[p])
        piece = piece + jnp.where(lanes == part_width + at, gate_part, 0.0)
        piece = piece.astype(BF)
        for s in range(sources):
            pieces_s[s, p, step] = piece[s * capacity : (s + 1) * capacity]

    @pl.when(step == steps - 1)
    def combine():
        for s in range(sources):
            picks = [choice(s, first + e).astype(F32).astype(BF) for e in range(many)]
            pick = jnp.concatenate(picks, axis=0)
            out = out_own if s < sources // 2 else out_far
            for p in range(parts):
                flat = pieces_s[s, p].reshape(many * capacity, padded)
                place = lax.rem(head_at + p, parts)
                out[place, s % (sources // 2)] = tdot(pick, flat).astype(BF)


def expert_work(rows, grads, weights_own, weights_far, places_here, capacity, total_experts, parts):
    sources = len(rows)
    tokens, wide = rows[0].shape
    padded = wide // parts
    many = weights_far[0].shape[0]
    part_width, hidden_width = weights_own[0].shape[1:]
    token_spec = pl.BlockSpec((tokens, wide), lambda e, p: (0, 0))
    wide_own = pl.BlockSpec((1, part_width, hidden_width), lambda e, p: (p[3] + e, 0, 0))
    wide_far = pl.BlockSpec((1, part_width, hidden_width), lambda e, p: (e, 0, 0))
    down_own = pl.BlockSpec((1, hidden_width, part_width), lambda e, p: (p[3] + e, 0, 0))
    down_far = pl.BlockSpec((1, hidden_width, part_width), lambda e, p: (e, 0, 0))
    out_shape = (parts, sources // 2, tokens, padded)
    out_spec = pl.BlockSpec(out_shape, lambda e, p: (0, 0, 0, 0))
    slots = sources * capacity
    (gate_own, up_own, down_own_w), (gate_far, up_far, down_far_w) = weights_own, weights_far
    return pl.pallas_call(
        functools.partial(experts_kernel, capacity, part_width, sources),
        grid_spec=pltpu.PrefetchScalarGridSpec(
            num_scalar_prefetch=1,
            grid=(many,),
            in_specs=[token_spec] * (2 * sources)
            + [wide_own, wide_far, wide_own, wide_far, down_own, down_far],
            out_specs=[out_spec, out_spec],
            scratch_shapes=[
                pltpu.VMEM((parts, padded, hidden_width), BF),
                pltpu.VMEM((parts, padded, hidden_width), BF),
                pltpu.VMEM((parts, hidden_width, padded), BF),
                pltpu.VMEM((many, slots, wide), BF),
                pltpu.VMEM((many, slots, wide), BF),
                pltpu.VMEM((sources, parts, many, capacity, padded), BF),
                pltpu.VMEM((sources, total_experts, tokens), F32),
                pltpu.VMEM((sources, total_experts, tokens), F32),
            ],
        ),
        out_shape=[jax.ShapeDtypeStruct(out_shape, BF)] * 2,
        compiler_params=pltpu.CompilerParams(vmem_limit_bytes=60 * 1024 * 1024),
        name="expert_work",
    )(
        places_here, *rows, *grads,
        gate_own, gate_far, up_own, up_far, down_own_w, down_far_w,
    )


def swapped(x, axis):
    return lax.ppermute(x, axis, [(0, 1), (1, 0)])


def turned(x, axis, by):
    count = lax.axis_size(axis)
    return lax.ppermute(x, axis, [(i, (i + by) % count) for i in range(count)])


def shifted(x, axis, by):
    count = lax.axis_size(axis)
    pairs = [(i, i + by) for i in range(count) if 0 <= i + by < count]
    return lax.ppermute(x, axis, pairs)


def apply_map(transfer, carried, state):
    return (
        lax.dot_general(
            transfer.astype(BF),
            state.astype(BF),
            (((2,), (1,)), ((0,), (0,))),
            preferred_element_type=F32,
        )
        + carried
    )


def split_wide(matrix, parts, padded):
    rows, wide = matrix.shape
    cut = matrix.reshape(rows, parts, wide // parts)
    cut = jnp.pad(cut, ((0, 0), (0, 0), (0, padded - wide // parts)))
    return cut.reshape(rows, parts * padded)


def per_device(
    queries,
    key_input,
    value_input,
    log_decay,
    write_rate,
    start_state,
    out_grad,
    end_grad,
    moe_input,
    moe_grad,
    expert_ids,
    gate_weights,
    gate_matrix,
    up_matrix,
    down_matrix,
):
    sections = lax.axis_size("ctx")
    position = lax.axis_index("ctx")
    parts = lax.axis_size("fsdp")
    core = lax.axis_index("fsdp")
    head_count = lax.axis_size("head")
    head_at = lax.axis_index("head")

    token_count, top_count = expert_ids.shape
    experts_here = gate_matrix.shape[0]
    many = experts_here // parts
    total_experts = experts_here * sections
    capacity = 3 * token_count // 8
    part_width = gate_matrix.shape[1]
    padded = -(-(part_width + total_experts) // 128) * 128

    far_at = (1 - core) * many
    weights_far = [
        swapped(lax.dynamic_slice_in_dim(w, far_at, many, 0), "fsdp")
        for w in (gate_matrix, up_matrix, down_matrix)
    ]

    named = expert_ids[:, :, None] == lax.iota(jnp.int32, total_experts)[None, None, :]
    dense = jnp.sum(jnp.where(named, gate_weights[:, :, None], 0.0), axis=1).astype(BF)
    spare = jnp.zeros((token_count, padded - part_width - total_experts), BF)
    rows_own = jnp.concatenate(
        [
            moe_input[:, :part_width],
            dense,
            spare,
            split_wide(moe_input[:, part_width:], parts - 1, padded),
        ],
        axis=1,
    )
    grads_own = split_wide(moe_grad.astype(BF), parts, padded)
    rows_all = [rows_own] + [turned(rows_own, "ctx", s) for s in range(1, sections)]
    grads_all = [grads_own] + [turned(grads_own, "ctx", s) for s in range(1, sections)]
    rows_all = rows_all + [swapped(r, "fsdp") for r in rows_all]
    grads_all = grads_all + [swapped(r, "fsdp") for r in grads_all]

    transfer, carried, own_grad, *saved = section_maps(
        queries, key_input, value_input, log_decay, write_rate, out_grad
    )
    entry_state, exit_grad = start_state, end_grad
    backward = jnp.swapaxes(transfer, 1, 2)
    for _ in range(sections - 1):
        leaving = apply_map(transfer, carried, entry_state).astype(BF)
        entering = apply_map(backward, own_grad, exit_grad).astype(BF)
        arrived = shifted(leaving, "ctx", 1).astype(F32)
        arrived_grad = shifted(entering, "ctx", -1).astype(F32)
        entry_state = jnp.where(position == 0, start_state, arrived)
        exit_grad = jnp.where(position == sections - 1, end_grad, arrived_grad)

    places_here = jnp.stack(
        [core, head_at, position * experts_here + core * many, core * many]
    ).astype(jnp.int32)
    out_own, out_far = expert_work(
        rows_all,
        grads_all,
        (gate_matrix, up_matrix, down_matrix),
        weights_far,
        places_here,
        capacity,
        total_experts,
        parts,
    )
    gradients = section_grads(
        queries, key_input, value_input, write_rate, out_grad, saved, entry_state, exit_grad
    )

    summed = out_own.astype(F32) + swapped(out_far, "fsdp").astype(F32)
    if head_count == parts:
        summed = summed[0] + swapped(summed[1].astype(BF), "head").astype(F32)
        pieces = summed.astype(BF)
        back = pieces[0].astype(F32)
        for s in range(1, sections):
            back = back + turned(pieces[s], "ctx", sections - s).astype(F32)
        input_grads = back[:, :part_width]
        gates = back[:, part_width : part_width + total_experts]
    else:
        order = (jnp.arange(parts) + head_at) % parts
        summed = summed[order].astype(BF)
        wide = jnp.concatenate([summed[p, :, :, :part_width] for p in range(parts)], axis=-1)
        wide = lax.psum_scatter(wide, "head", scatter_dimension=2, tiled=True)
        gates = lax.psum(summed[0, :, :, part_width : part_width + total_experts], "head")
        pieces = jnp.concatenate([wide, gates], axis=-1)
        back = pieces[0].astype(F32)
        for s in range(1, sections):
            back = back + turned(pieces[s], "ctx", sections - s).astype(F32)
        input_grads = back[:, : wide.shape[-1]]
        gates = back[:, wide.shape[-1] :]
    slots_here = top_count // head_count
    ids_here = lax.dynamic_slice_in_dim(expert_ids, head_at * slots_here, slots_here, 1)
    named = ids_here[:, :, None] == lax.iota(jnp.int32, total_experts)[None, None, :]
    gate_grads = jnp.sum(jnp.where(named, gates[:, None, :], 0.0), axis=-1)
    return (*gradients[:5], gradients[5][None], input_grads, gate_grads)


def solution(mesh):
    in_specs = (
        P(("groups", "ctx"), ("head", "fsdp")),
        P(("groups", "ctx"), ("head", "fsdp")),
        P(("groups", "ctx"), ("head", "fsdp")),
        P(("groups", "ctx"), ("head", "fsdp")),
        P(("groups", "ctx"), ("head", "fsdp")),
        P(("groups", "head", "fsdp"), None, None),
        P(("groups", "ctx"), ("head", "fsdp")),
        P(("groups", "head", "fsdp"), None, None),
        P(("groups", "ctx", "fsdp"), None),
        P(("groups", "ctx", "fsdp"), None),
        P(("groups", "ctx", "fsdp"), None),
        P(("groups", "ctx", "fsdp"), None),
        P("ctx", "fsdp", "head"),
        P("ctx", "fsdp", "head"),
        P("ctx", "head", "fsdp"),
    )
    out_specs = (
        P(("groups", "ctx"), ("head", "fsdp")),
        P(("groups", "ctx"), ("head", "fsdp")),
        P(("groups", "ctx"), ("head", "fsdp")),
        P(("groups", "ctx"), ("head", "fsdp")),
        P(("groups", "ctx"), ("head", "fsdp")),
        P(("groups", "ctx"), ("head", "fsdp"), None, None),
        P(("groups", "ctx", "fsdp"), "head"),
        P(("groups", "ctx", "fsdp"), "head"),
    )
    return jax.shard_map(
        per_device, mesh=mesh, in_specs=in_specs, out_specs=out_specs, check_vma=False
    )
```

```python
import functools

import jax
import jax.numpy as jnp
from jax import lax
from jax.experimental import pallas as pl
from jax.experimental.pallas import tpu as pltpu
from jax.sharding import PartitionSpec as P

BF = jnp.bfloat16
F32 = jnp.float32
VMEM_BYTES = 62 * 1024 * 1024


def dot(a, b):
    return lax.dot_general(
        a.astype(BF), b.astype(BF), (((1,), (0,)), ((), ())), preferred_element_type=F32
    )


def dot_t(a, b):
    return lax.dot_general(
        a.astype(BF), b.astype(BF), (((1,), (1,)), ((), ())), preferred_element_type=F32
    )


def tdot(a, b):
    return lax.dot_general(
        a.astype(BF), b.astype(BF), (((0,), (0,)), ((), ())), preferred_element_type=F32
    )


def halves(x, axis):
    high = x.astype(BF)
    return jnp.concatenate([high, (x - high.astype(F32)).astype(BF)], axis=axis)


def places(size, axis):
    return lax.broadcasted_iota(jnp.int32, (size, size), axis)


def column(matrix, at):
    lanes = lax.broadcasted_iota(jnp.int32, matrix.shape, 1)
    return jnp.sum(jnp.where(lanes == at, matrix, 0.0), axis=1, keepdims=True)


def to_column(row):
    size = row.shape[1]
    spread = jnp.broadcast_to(row, (size, size))
    return jnp.sum(jnp.where(places(size, 0) == places(size, 1), spread, 0.0), axis=1, keepdims=True)


def inverse_less_one(scores):
    size = scores[0].shape[0]
    rows, cols = places(size, 0), places(size, 1)
    eye = (rows == cols).astype(F32)
    span, off = 1, None
    while span < size:
        joins = (rows // (2 * span) == cols // (2 * span)) & (rows // span != cols // span)
        parts = [jnp.where(joins, a, 0.0).astype(BF) for a in scores]
        if off is None:
            off = [-p.astype(F32) for p in parts]
        else:
            full = [(o + eye).astype(BF) for o in off]
            half = [dot(p, f) for p, f in zip(parts, full)]
            off = [o - dot(f, h) for o, f, h in zip(off, full, half)]
        span *= 2
    return off


def maps_kernel(
    chunk,
    width,
    heads_step,
    first,
    given,
    query_ref,
    key_ref,
    value_ref,
    decay_ref,
    rate_ref,
    grad_ref,
    *refs,
):
    (
        transfer_ref,
        carried_ref,
        own_ref,
        cum_ref,
        query_l_ref,
        key_l_ref,
        back_ref,
        lower_ref,
        score_ref,
    ) = refs[given:]
    tokens = query_ref.shape[0]
    chunks = tokens // chunk
    rows, cols = places(chunk, 0), places(chunk, 1)
    tri = (rows >= cols).astype(BF)
    tri = jnp.concatenate([tri, tri], axis=1)
    units = [(h, i) for h in range(heads_step) for i in range(chunks)]
    first = first + pl.program_id(0) * heads_step
    rate_cols = jnp.transpose(rate_ref[...])
    rates = [column(rate_cols, first + h) for h in range(heads_step)]

    def part(ref, unit):
        h, i = unit
        return ref[i * chunk : (i + 1) * chunk, h * width : (h + 1) * width]

    def unit_rows(x):
        return x * lax.rsqrt(jnp.sum(x * x, axis=-1, keepdims=True) + 1e-06)

    cums = [dot(tri, halves(part(decay_ref, u), 0)) for u in units]
    queries = [unit_rows(part(query_ref, u)) for u in units]
    keys = [unit_rows(part(key_ref, u)) for u in units]
    values = [part(value_ref, u) for u in units]
    middles = [0.5 * c[chunk - 1 : chunk, :] for c in cums]
    lifts = [jnp.exp(c - m) for c, m in zip(cums, middles)]
    sinks = [jnp.exp(m - c) for c, m in zip(cums, middles)]
    key_l = [(k * e).astype(BF) for k, e in zip(keys, lifts)]
    query_l = [(q * e).astype(BF) for q, e in zip(queries, lifts)]
    back = [
        (k * e * rates[h][i * chunk : (i + 1) * chunk]).astype(BF)
        for k, e, (h, i) in zip(keys, sinks, units)
    ]
    both = [dot_t(jnp.concatenate([k, q], axis=0), b) for k, q, b in zip(key_l, query_l, back)]
    key_scores = [jnp.where(rows > cols, s[:chunk], 0.0) for s in both]
    scores = [jnp.where(rows >= cols, s[chunk:], 0.0).astype(BF) for s in both]
    lower = [o.astype(BF) for o in inverse_less_one(key_scores)]
    wide = [jnp.concatenate([k, v.astype(BF)], axis=1) for k, v in zip(key_l, values)]
    solved = [
        dot(o, w) + jnp.concatenate([k.astype(F32), v], axis=1)
        for o, w, k, v in zip(lower, wide, key_l, values)
    ]
    solved = [s.astype(BF) for s in solved]
    stepped = [tdot(b, s) for b, s in zip(back, solved)]
    reads = [q.astype(F32) - dot(p, s[:, :width]) for q, p, s in zip(query_l, scores, solved)]
    mids = [to_column(jnp.exp(m)) for m in middles]
    owns = [m * tdot(r, part(grad_ref, u)) for m, r, u in zip(mids, reads, units)]
    for n, u in enumerate(units):
        h, i = u
        span = slice(i * chunk, (i + 1) * chunk)
        lanes = slice(h * width, (h + 1) * width)
        cum_ref[span, lanes] = cums[n]
        query_l_ref[span, lanes] = query_l[n]
        key_l_ref[span, lanes] = key_l[n]
        back_ref[span, lanes] = back[n]
        lower_ref[h, span, :] = lower[n]
        score_ref[h, span, :] = scores[n]
    eye = (places(width, 0) == places(width, 1)).astype(F32)
    for h in range(heads_step):
        state = None
        for i in range(chunks):
            n = h * chunks + i
            mid, step = mids[n], stepped[n][:, :width]
            entering = jnp.concatenate([eye, jnp.zeros_like(eye)], axis=1) if i == 0 else state
            scaled = mid * entering
            moved = scaled - dot(step, scaled)
            carried = jnp.concatenate([jnp.zeros_like(eye), stepped[n][:, width:]], axis=1)
            state = mid * (moved + carried)
        transfer_ref[h] = state[:, :width].astype(BF)
        carried_ref[h] = state[:, width:].astype(BF)
        total = owns[h * chunks + chunks - 1]
        for i in range(chunks - 2, -1, -1):
            n = h * chunks + i
            scaled = mids[n] * total
            total = owns[n] + mids[n] * (scaled - tdot(stepped[n][:, :width], scaled))
        own_ref[h] = total.astype(BF)


def grads_kernel(
    chunk,
    width,
    heads_step,
    place_ref,
    query_ref,
    key_ref,
    value_ref,
    rate_ref,
    grad_ref,
    cum_ref,
    query_l_ref,
    key_l_ref,
    back_ref,
    lower_ref,
    score_ref,
    start_ref,
    end_ref,
    *refs,
):
    arrived_refs, refs, rate_s = refs[:-7], refs[-7:-1], refs[-1]
    (
        query_grad_ref,
        key_grad_ref,
        value_grad_ref,
        decay_grad_ref,
        rate_grad_ref,
        state_grad_ref,
    ) = refs
    position, last = place_ref[0], len(arrived_refs)

    def arrived(own_ref, h, turn):
        state = own_ref[h]
        for r, ref in enumerate(arrived_refs):
            state = jnp.where(position == turn(r + 1), ref[h].astype(F32), state)
        return state

    tokens = query_ref.shape[0]
    chunks = tokens // chunk
    rows, cols = places(chunk, 0), places(chunk, 1)
    tri = (rows <= cols).astype(BF)
    tri = jnp.concatenate([tri, tri], axis=1)
    first = pl.program_id(0) * heads_step
    heads = range(heads_step)
    rate_cols = jnp.transpose(rate_ref[...])
    rates = [column(rate_cols, first + h) for h in heads]

    def part(ref, h, i):
        return ref[i * chunk : (i + 1) * chunk, h * width : (h + 1) * width]

    def mat(ref, h, i):
        return ref[h, i * chunk : (i + 1) * chunk, :]

    cums = {(h, i): part(cum_ref, h, i) for i in range(chunks) for h in heads}
    middles = {u: 0.5 * c[chunk - 1 : chunk, :] for u, c in cums.items()}
    mids = {u: to_column(jnp.exp(m)) for u, m in middles.items()}
    states = {(h, 0): arrived(start_ref, h, lambda r: r) for h in heads}
    scaled, updates = {}, {}
    for i in range(chunks):
        for h in heads:
            u = (h, i)
            scaled[u] = mids[u] * states[u]
        rests = [part(value_ref, h, i) - dot(part(key_l_ref, h, i), scaled[h, i]) for h in heads]
        for h in heads:
            updates[h, i] = (rests[h] + dot(mat(lower_ref, h, i), rests[h])).astype(BF)
        for h in heads:
            moved = scaled[h, i] + tdot(part(back_ref, h, i), updates[h, i])
            states[h, i + 1] = mids[h, i] * moved
    out = {(h, chunks): arrived(end_ref, h, lambda r: last - r) for h in heads}
    rest_grads, lifted, out_grads = {}, {}, {}
    for i in range(chunks - 1, -1, -1):
        update_grads = []
        for h in heads:
            lifted[h, i] = mids[h, i] * out[h, i + 1]
            out_grads[h, i] = part(grad_ref, h, i).astype(BF)
            got = tdot(mat(score_ref, h, i), out_grads[h, i])
            update_grads.append(got + dot(part(back_ref, h, i), lifted[h, i]))
        for h in heads:
            rest = update_grads[h] + tdot(mat(lower_ref, h, i), update_grads[h])
            value_grad_ref[i * chunk : (i + 1) * chunk, h * width : (h + 1) * width] = rest
            rest_grads[h, i] = rest.astype(BF)
        for h in heads:
            left = jnp.concatenate([part(query_l_ref, h, i), part(key_l_ref, h, i)], axis=0)
            right = jnp.concatenate([out_grads[h, i], -rest_grads[h, i]], axis=0)
            out[h, i] = mids[h, i] * (lifted[h, i] + tdot(left, right))
    for h in heads:
        state_grad_ref[h] = out[h, 0]
    units = [(h, i) for i in range(chunks) for h in heads]
    joint = [jnp.concatenate([-rest_grads[u], out_grads[u]], axis=0) for u in units]
    pairs = [dot_t(j, updates[u]) for j, u in zip(joint, units)]
    key_pairs = [jnp.where(rows > cols, p[:chunk], 0.0).astype(BF) for p in pairs]
    query_pairs = [jnp.where(rows >= cols, p[chunk:], 0.0).astype(BF) for p in pairs]
    pairs = [jnp.concatenate([k, q], axis=0) for k, q in zip(key_pairs, query_pairs)]
    left_grads = [
        dot(p, part(back_ref, *u)) + dot_t(j, scaled[u]) for p, j, u in zip(pairs, joint, units)
    ]
    back_grads = [
        tdot(p, jnp.concatenate([part(key_l_ref, *u), part(query_l_ref, *u)], axis=0))
        + dot_t(updates[u], lifted[u])
        for p, u in zip(pairs, units)
    ]
    ones = jnp.ones((8, 2 * width), BF)
    crossing = [
        dot_t(ones, halves(out[h, i + 1] * states[h, i + 1], 1))[:1] for h, i in units
    ]
    slopes = [
        part(key_l_ref, *u).astype(F32) * l[:chunk]
        + part(query_l_ref, *u).astype(F32) * l[chunk:]
        - part(back_ref, *u).astype(F32) * b
        for u, l, b in zip(units, left_grads, back_grads)
    ]
    decays = [dot(tri, halves(s, 0)) + c for s, c in zip(slopes, crossing)]
    lanes = lax.broadcasted_iota(jnp.int32, (chunk, rate_s.shape[1]), 1)
    for n, (h, i) in enumerate(units):
        span = slice(i * chunk, (i + 1) * chunk)
        at = slice(h * width, (h + 1) * width)
        decay_grad_ref[span, at] = decays[n]
        gap = cums[h, i] - middles[h, i]
        lift, sink = jnp.exp(gap), jnp.exp(-gap)
        rate = rates[h][span]
        query, key = query_ref[span, at], key_ref[span, at]
        query_norm = lax.rsqrt(jnp.sum(query * query, axis=-1, keepdims=True) + 1e-06)
        key_norm = lax.rsqrt(jnp.sum(key * key, axis=-1, keepdims=True) + 1e-06)
        query, key = query * query_norm, key * key_norm
        query_grad = left_grads[n][chunk:] * lift
        sunk = back_grads[n] * sink
        key_grad = left_grads[n][:chunk] * lift + rate * sunk
        rate_grad = jnp.sum(sunk * key, axis=-1, keepdims=True)
        query_grad_ref[span, at] = query_norm * (
            query_grad - query * jnp.sum(query * query_grad, axis=-1, keepdims=True)
        )
        key_grad_ref[span, at] = key_norm * (
            key_grad - key * jnp.sum(key * key_grad, axis=-1, keepdims=True)
        )
        rate_s[span, :] = jnp.where(lanes == first + h, rate_grad, rate_s[span, :])

    @pl.when(pl.program_id(0) == pl.num_programs(0) - 1)
    def finish():
        rate_grad_ref[...] = jnp.transpose(rate_s[...])[: rate_grad_ref.shape[0]]


def specs_of(tokens, width, chunk, heads_step, rate_heads, skip=0):
    lanes = pl.BlockSpec((tokens, heads_step * width), lambda h, *p: (0, skip + h))
    rate = pl.BlockSpec((rate_heads, tokens), lambda h, *p: (0, 0))
    square = pl.BlockSpec((heads_step, tokens, chunk), lambda h, *p: (skip + h, 0, 0))
    state = pl.BlockSpec((heads_step, width, width), lambda h, *p: (skip + h, 0, 0))
    return lanes, rate, square, state


def section_maps(
    queries, key_input, value_input, log_decay, write_rate, out_grad, first, heads, into=()
):
    heads_all, tokens = write_rate.shape
    width = queries.shape[1] // heads_all
    chunk = min(128, tokens)
    heads_step = 2 if heads % 2 == 0 and first % 2 == 0 else 1
    lanes, rate, square, state = specs_of(
        tokens, width, chunk, heads_step, heads_all, first // heads_step
    )
    shape = jax.ShapeDtypeStruct
    return pl.pallas_call(
        functools.partial(maps_kernel, chunk, width, heads_step, first, len(into)),
        grid=(heads // heads_step,),
        in_specs=[lanes, lanes, lanes, lanes, rate, lanes]
        + [pl.BlockSpec(memory_space=pl.ANY)] * len(into),
        out_specs=[state, state, state, lanes, lanes, lanes, lanes, square, square],
        out_shape=[shape((heads_all, width, width), BF)] * 3
        + [shape(queries.shape, F32)]
        + [shape(queries.shape, BF)] * 3
        + [shape((heads_all, tokens, chunk), BF)] * 2,
        input_output_aliases={6 + n: n for n in range(len(into))},
        compiler_params=pltpu.CompilerParams(vmem_limit_bytes=VMEM_BYTES),
        cost_estimate=pl.CostEstimate(flops=10**8, bytes_accessed=10**7, transcendentals=0),
        name="section_maps",
    )(queries, key_input, value_input, log_decay, write_rate, out_grad, *into)


def section_grads(
    place, queries, key_input, value_input, write_rate, out_grad, saved, ends, arrivals
):
    heads, tokens = write_rate.shape
    width = queries.shape[1] // heads
    chunk = min(128, tokens)
    heads_step = 2 if heads % 2 == 0 else 1
    lanes, rate, square, state = specs_of(tokens, width, chunk, heads_step, heads)
    shape = jax.ShapeDtypeStruct
    return pl.pallas_call(
        functools.partial(grads_kernel, chunk, width, heads_step),
        grid_spec=pltpu.PrefetchScalarGridSpec(
            num_scalar_prefetch=1,
            grid=(heads // heads_step,),
            in_specs=[lanes, lanes, lanes, rate, lanes]
            + [lanes] * 4
            + [square] * 2
            + [state] * (2 + len(arrivals)),
            out_specs=[lanes, lanes, lanes, lanes, rate, state],
            scratch_shapes=[pltpu.VMEM((tokens, 128), F32)],
        ),
        out_shape=[shape(queries.shape, F32)] * 4
        + [shape((heads, tokens), F32), shape((heads, width, width), F32)],
        compiler_params=pltpu.CompilerParams(vmem_limit_bytes=VMEM_BYTES),
        cost_estimate=pl.CostEstimate(flops=10**8, bytes_accessed=10**7, transcendentals=0),
        name="section_grads",
    )(place, queries, key_input, value_input, write_rate, out_grad, *saved, *ends, *arrivals)


def hop_kernel(backward_at, place_ref, transfer_ref, carried_ref, own_ref, state_ref, out_ref):
    heads = transfer_ref.shape[0]

    @pl.when(place_ref[0] == backward_at)
    def backward():
        for h in range(heads):
            out_ref[h] = (tdot(transfer_ref[h], state_ref[h]) + own_ref[h]).astype(BF)

    @pl.when(place_ref[0] != backward_at)
    def forward():
        for h in range(heads):
            out_ref[h] = (dot(transfer_ref[h], state_ref[h]) + carried_ref[h]).astype(BF)


def hop(place, transfer, carried, own_grad, state, turn, sections):
    spec = pl.BlockSpec(state.shape, lambda i, p: (0, 0, 0))
    leaving = pl.pallas_call(
        functools.partial(hop_kernel, sections - turn),
        grid_spec=pltpu.PrefetchScalarGridSpec(
            num_scalar_prefetch=1, grid=(1,), in_specs=[spec] * 4, out_specs=spec
        ),
        out_shape=jax.ShapeDtypeStruct(state.shape, BF),
        compiler_params=pltpu.CompilerParams(vmem_limit_bytes=VMEM_BYTES),
        cost_estimate=pl.CostEstimate(flops=10**8, bytes_accessed=10**6, transcendentals=0),
        name="hop",
    )(place, transfer, carried, own_grad, state)
    pairs = [(turn - 1, turn), (sections - turn, sections - turn - 1)]
    return lax.ppermute(leaving, "ctx", pairs)


def experts_kernel(capacity, part_width, order, place_ref, *refs):
    sources = len(order)
    own_ref, came_refs, other_refs = refs[0], refs[1:sources], refs[sources : 2 * sources - 1]
    weight_refs, refs = refs[2 * sources - 1 : 2 * sources + 5], refs[2 * sources + 5 :]
    keep_ref, send_refs, scratch = refs[0], refs[1:3], refs[3:]
    weights_s, tokens_s, pieces_s, ranks_s, gates_s, sems = scratch
    step, steps = pl.program_id(0), pl.num_programs(0)
    mine, head_at, first, came_is = place_ref[0], place_ref[1], place_ref[2], place_ref[3]
    tokens = own_ref.shape[0]
    wide, hidden_width = weights_s.shape[2:]
    padded = wide // 2
    experts = ranks_s.shape[1]
    many = tokens_s.shape[1]

    def weight_copies(expert, slot):
        for m in range(3):
            for far in range(2):
                part = mine if far == 0 else 1 - mine
                at = pl.multiple_of(part * padded, 128)
                yield pltpu.make_async_copy(
                    weight_refs[2 * m + far].at[expert],
                    weights_s.at[slot, m, pl.ds(at, part_width)],
                    sems.at[slot, 2 * m + far],
                )

    def choice(source, at):
        rank = ranks_s[source, pl.ds(at, 1), :]
        slot = lax.broadcasted_iota(jnp.int32, (capacity, tokens), 0).astype(F32)
        return slot == rank

    def choices(source):
        picks = [choice(source, first + e).astype(F32).astype(BF) for e in range(many)]
        return jnp.concatenate(picks, axis=0)

    slot = lax.rem(step, 2)

    @pl.when(step == 0)
    def dispatch():
        for copy in weight_copies(0, 0):
            copy.start()
        blank = jnp.zeros((padded - part_width, hidden_width), BF)
        for n in range(2):
            for m in range(3):
                weights_s[n, m, part_width:padded] = blank
                weights_s[n, m, padded + part_width :] = blank
        before = (places(tokens, 0) < places(tokens, 1)).astype(BF)
        for s, turn in enumerate(order):
            if turn == 0:
                came, other, kind = own_ref.at[:, :wide], own_ref.at[:, wide:], 0
            else:
                came, other, kind = came_refs[turn - 1], other_refs[turn - 1], came_is
            start = part_width // 128 * 128
            offset = part_width - start
            dense = jnp.transpose(came[:, start : start + 128].astype(F32))
            dense = dense[offset : offset + experts]
            named = dense > 0.0
            rank = dot(named.astype(F32), before)
            ranks_s[s] = jnp.where(named, rank, -1.0)
            gates_s[s] = dense
            pick = choices(s)
            for which, ref in ((kind, came), (1 - kind, other)):
                picked = dot(pick, ref[...]).astype(BF)
                for e in range(many):
                    span = slice(s * capacity, (s + 1) * capacity)
                    tokens_s[which, e, span] = picked[e * capacity : (e + 1) * capacity]

    @pl.when(step + 1 < steps)
    def prefetch():
        for copy in weight_copies(step + 1, 1 - slot):
            copy.start()

    for copy in weight_copies(step, slot):
        copy.wait()
    at = first + step
    gate_pre = dot(tokens_s[0, step], weights_s[slot, 0])
    up_pre = dot(tokens_s[0, step], weights_s[slot, 1])
    raw_grad = dot(tokens_s[1, step], weights_s[slot, 2])
    weight = jnp.concatenate(
        [
            jnp.sum(
                jnp.where(choice(s, at), gates_s[s, pl.ds(at, 1), :], 0.0), axis=1, keepdims=True
            )
            for s in range(sources)
        ],
        axis=0,
    )
    sigmoid = jax.nn.sigmoid(gate_pre)
    activated = gate_pre * sigmoid
    hidden = (activated * up_pre).astype(BF).astype(F32)
    gate_part = jnp.sum(hidden * raw_grad, axis=1, keepdims=True)
    scaled = raw_grad * weight
    gate_back = (scaled * up_pre * sigmoid * (1.0 + gate_pre * (1.0 - sigmoid))).astype(BF)
    up_back = (scaled * activated).astype(BF)
    piece = dot_t(gate_back, weights_s[slot, 0]) + dot_t(up_back, weights_s[slot, 1])
    lanes = lax.broadcasted_iota(jnp.int32, (1, wide), 1)
    here = (lanes == part_width + at) | (lanes == padded + part_width + at)
    piece = (piece + jnp.where(here, gate_part, 0.0)).astype(BF)
    for s in range(sources):
        pieces_s[s, step] = piece[s * capacity : (s + 1) * capacity]

    @pl.when(step == steps - 1)
    def combine():
        per = send_refs[0].shape[0]
        for s in range(sources):
            flat = pieces_s[s].reshape(many * capacity, wide)
            total = tdot(choices(s), flat).astype(BF)
            left, right = total[:, :padded], total[:, padded:]
            keep_ref[s] = jnp.where(head_at == 0, left, right)
            send_refs[s // per][s % per] = jnp.where(head_at == 0, right, left)


def expert_work(place, own, came, other, weights, capacity, total_experts, order):
    tokens, wide = came[0].shape
    many, part_width, hidden_width = weights[0].shape
    sources = len(order)
    padded = wide // 2
    whole = lambda x: pl.BlockSpec(x.shape, lambda e, p: (0,) * len(x.shape))
    shape = jax.ShapeDtypeStruct
    outs = [shape((n, tokens, padded), BF) for n in (sources, sources // 2, sources // 2)]
    token_args = (own, *came, *other)
    return pl.pallas_call(
        functools.partial(experts_kernel, capacity, part_width, order),
        grid_spec=pltpu.PrefetchScalarGridSpec(
            num_scalar_prefetch=1,
            grid=(many,),
            in_specs=[whole(x) for x in token_args]
            + [pl.BlockSpec(memory_space=pl.ANY)] * len(weights),
            out_specs=[whole(x) for x in outs],
            scratch_shapes=[
                pltpu.VMEM((2, 3, wide, hidden_width), BF),
                pltpu.VMEM((2, many, sources * capacity, wide), BF),
                pltpu.VMEM((sources, many, capacity, wide), BF),
                pltpu.VMEM((sources, total_experts, tokens), F32),
                pltpu.VMEM((sources, total_experts, tokens), F32),
                pltpu.SemaphoreType.DMA((2, 6)),
            ],
        ),
        out_shape=outs,
        compiler_params=pltpu.CompilerParams(vmem_limit_bytes=VMEM_BYTES),
        name="expert_work",
    )(place, *token_args, *weights)


def plain_call(kernel, name, out_shape, *args):
    return pl.pallas_call(
        kernel,
        out_shape=out_shape,
        compiler_params=pltpu.CompilerParams(vmem_limit_bytes=VMEM_BYTES),
        name=name,
    )(*args)


def head_sum_kernel(first, keep, got, *outs):
    for k, out in enumerate(outs):
        out[...] = (keep[first + k].astype(F32) + got[k].astype(F32)).astype(BF)


def home_kernel(part_width, experts, at_ref, ids_ref, *refs):
    pieces, (input_ref, gate_ref) = refs[:-2], refs[-2:]
    total = pieces[0][...].astype(F32)
    for piece in pieces[1:]:
        total = total + piece[...].astype(F32)
    total = jnp.transpose(total)
    input_ref[...] = total[:part_width]
    gates = total[part_width : part_width + experts]
    slots = gate_ref.shape[0]
    names = lax.broadcasted_iota(jnp.int32, gates.shape, 0)
    for j in range(slots):
        ids = ids_ref[pl.ds(at_ref[0] * slots + j, 1), :]
        gate_ref[j : j + 1, :] = jnp.sum(jnp.where(names == ids, gates, 0.0), axis=0, keepdims=True)


def swapped(x, axis):
    return lax.ppermute(x, axis, [(0, 1), (1, 0)])


def turned(x, axis, by):
    count = lax.axis_size(axis)
    return lax.ppermute(x, axis, [(i, (i + by) % count) for i in range(count)])


def pack_kernel(
    part_width, padded, which_ref, rows_ref, grads_ref, ids_ref, gates_ref, own_ref, sent_ref
):
    top, tokens = ids_ref.shape
    start = part_width // 128 * 128
    experts = lax.broadcasted_iota(jnp.int32, (128, tokens), 0) + (start - part_width)
    dense = jnp.zeros((128, tokens), F32)
    for j in range(top):
        named = experts == ids_ref[j : j + 1, :]
        dense = dense + jnp.where(named, gates_ref[j : j + 1, :], 0.0)
    dense = jnp.transpose(dense)
    lanes = lax.broadcasted_iota(jnp.int32, (tokens, 128), 1) + start
    wide = 2 * padded
    for n, ref in enumerate((rows_ref, grads_ref)):
        x = ref[...].astype(F32)
        x = jnp.concatenate([x, jnp.zeros((tokens, wide - x.shape[1]), F32)], axis=1)
        moved = pltpu.roll(x, padded - part_width, 1)
        tile = jnp.where(lanes < part_width, x[:, start : start + 128], dense)
        blank = jnp.zeros((tokens, padded - start - 128), F32)
        pieces = [x[:, :start], tile] + [blank] * (start + 128 < padded) + [moved[:, padded:]]
        packed = jnp.concatenate(pieces, axis=1).astype(BF)
        own_ref[:, n * wide : (n + 1) * wide] = packed

        @pl.when(which_ref[0] == n)
        def keep(packed=packed):
            sent_ref[...] = packed


def packed_tokens(first_is, rows, grads, ids, gates, part_width, padded):
    tokens = rows.shape[0]
    whole = lambda x: pl.BlockSpec(x.shape, lambda i, p: (0, 0))
    shapes = [jax.ShapeDtypeStruct((tokens, n * padded), BF) for n in (4, 2)]
    return pl.pallas_call(
        functools.partial(pack_kernel, part_width, padded),
        grid_spec=pltpu.PrefetchScalarGridSpec(
            num_scalar_prefetch=1,
            grid=(1,),
            in_specs=[whole(x) for x in (rows, grads, ids, gates)],
            out_specs=[whole(x) for x in shapes],
        ),
        out_shape=shapes,
        compiler_params=pltpu.CompilerParams(vmem_limit_bytes=VMEM_BYTES),
        name="packed_tokens",
    )(first_is, rows, grads, ids, gates)


def per_device(
    queries,
    key_input,
    value_input,
    log_decay,
    write_rate,
    start_state,
    out_grad,
    end_grad,
    moe_input,
    moe_grad,
    expert_ids,
    gate_weights,
    gate_matrix,
    up_matrix,
    down_matrix,
):
    sections = lax.axis_size("ctx")
    position = lax.axis_index("ctx")
    parts = lax.axis_size("fsdp")
    core = lax.axis_index("fsdp")
    head_count = lax.axis_size("head")
    head_at = lax.axis_index("head")

    token_count, top_count = expert_ids.shape
    experts_here = gate_matrix.shape[0]
    total_experts = experts_here * sections
    capacity = 3 * token_count // 8
    part_width = gate_matrix.shape[1]
    padded = -(-(part_width + total_experts) // 128) * 128

    turns = range(1, sections)
    near = [s for s in turns if s in (1, sections - 1)]
    far = [s for s in turns if s not in near]
    order = far + near + [0]
    came_is = head_at if head_count == 2 else 0 * head_at
    came_is = came_is.astype(jnp.int32)
    place = jnp.reshape(position, (1,)).astype(jnp.int32)
    recurrent = (queries, key_input, value_input, log_decay, write_rate.T, out_grad)
    heads_here = write_rate.shape[1]
    weights_own = [gate_matrix, up_matrix, jnp.swapaxes(down_matrix, 1, 2)]
    came, other, weights_far = {}, {}, [None] * 3

    def fetch_other(s):
        if head_count == 2:
            other[s] = swapped(came[s], "head")
        else:
            other[s] = turned(own[:, own.shape[1] // 2 :], "ctx", s)

    own, sent = packed_tokens(
        came_is.reshape(1), moe_input, moe_grad, expert_ids.T, gate_weights.T, part_width, padded
    )
    sent, recurrent, weights_own = lax.optimization_barrier((sent, recurrent, weights_own))
    for s in near:
        came[s] = turned(sent, "ctx", s)
    weights_far[0] = swapped(weights_own[0], "fsdp")
    first_maps = section_maps(*recurrent, 0, heads_here // 2)
    came, weights_far[0], first_maps, recurrent, sent, weights_own = lax.optimization_barrier(
        (came, weights_far[0], first_maps, recurrent, sent, weights_own)
    )
    for s in far:
        came[s] = turned(sent, "ctx", s)
    for s in near:
        fetch_other(s)
    weights_far[1] = swapped(weights_own[1], "fsdp")
    last_maps = section_maps(
        *recurrent, heads_here // 2, heads_here - heads_here // 2, into=first_maps
    )
    came, other, weights_far[1], last_maps, weights_own = lax.optimization_barrier(
        (came, other, weights_far[1], last_maps, weights_own)
    )
    for s in far:
        fetch_other(s)
    weights_far[2] = swapped(weights_own[2], "fsdp")
    transfer, carried, own_grad, *saved = last_maps
    state = jnp.where(position == 0, start_state, end_grad).astype(BF)
    state = hop(place, transfer, carried, own_grad, state, 1, sections)
    arrivals = [state]
    if sections > 2:
        other, state = lax.optimization_barrier((other, state))
        state = hop(place, transfer, carried, own_grad, state, 2, sections)
        arrivals.append(state)
    expert_place = jnp.stack([core, head_at, position * experts_here, came_is]).astype(jnp.int32)
    weights = [w for pair in zip(weights_own, weights_far) for w in pair]
    keep, *sends = expert_work(
        expert_place,
        own,
        [came[s] for s in turns],
        [other[s] for s in turns],
        weights,
        capacity,
        total_experts,
        order,
    )
    for turn in range(3, sections):
        state = hop(place, transfer, carried, own_grad, state, turn, sections)
        arrivals.append(state)
    gradients = section_grads(
        place,
        queries,
        key_input,
        value_input,
        write_rate.T,
        out_grad,
        saved,
        (start_state, end_grad),
        arrivals,
    )

    if head_count == 2:
        shape = jax.ShapeDtypeStruct
        per = len(order) // 2
        block = (token_count, padded)
        pieces = []
        for n, send in enumerate(sends):
            sums = plain_call(
                functools.partial(head_sum_kernel, n * per),
                "head_sum",
                [shape(block, BF)] * per,
                keep, swapped(send, "head"),
            )
            for turn, piece in zip(order[n * per : (n + 1) * per], sums):
                pieces.append(turned(piece, "ctx", sections - turn) if turn else piece)
        whole = lambda x: pl.BlockSpec(x.shape, lambda i, p: (0, 0))
        outs = [shape((part_width, token_count), F32), shape((top_count // 2, token_count), F32)]
        home_args = (expert_ids.T, *pieces)
        input_grads, gate_grads = pl.pallas_call(
            functools.partial(home_kernel, part_width, total_experts),
            grid_spec=pltpu.PrefetchScalarGridSpec(
                num_scalar_prefetch=1,
                grid=(1,),
                in_specs=[whole(x) for x in home_args],
                out_specs=[whole(x) for x in outs],
            ),
            out_shape=outs,
            compiler_params=pltpu.CompilerParams(vmem_limit_bytes=VMEM_BYTES),
            name="home",
        )(head_at.astype(jnp.int32).reshape(1), *home_args)
        input_grads, gate_grads = input_grads.T, gate_grads.T
    else:
        sent_back = jnp.concatenate(sends, axis=0)
        halves_in = [jnp.where(head_at == 0, keep, sent_back), jnp.where(head_at == 0, sent_back, keep)]
        wide = jnp.concatenate([x[:, :, :part_width] for x in halves_in], axis=-1)
        wide = lax.psum_scatter(wide, "head", scatter_dimension=2, tiled=True)
        gates = lax.psum(keep[:, :, part_width : part_width + total_experts], "head")
        pieces = jnp.concatenate([wide, gates], axis=-1)
        back = 0.0
        for piece, turn in zip(pieces, order):
            back = back + (turned(piece, "ctx", sections - turn) if turn else piece).astype(F32)
        input_grads, gates = back[:, : wide.shape[-1]], back[:, wide.shape[-1] :]
        slots_here = top_count // head_count
        ids_here = lax.dynamic_slice_in_dim(expert_ids, head_at * slots_here, slots_here, 1)
        named = ids_here[:, :, None] == lax.iota(jnp.int32, total_experts)[None, None, :]
        gate_grads = jnp.sum(jnp.where(named, gates[:, None, :], 0.0), axis=-1)
    return (*gradients[:4], gradients[4].T, gradients[5][None], input_grads, gate_grads)


def solution(mesh):
    in_specs = (
        P(("groups", "ctx"), ("head", "fsdp")),
        P(("groups", "ctx"), ("head", "fsdp")),
        P(("groups", "ctx"), ("head", "fsdp")),
        P(("groups", "ctx"), ("head", "fsdp")),
        P(("groups", "ctx"), ("head", "fsdp")),
        P(("groups", "head", "fsdp"), None, None),
        P(("groups", "ctx"), ("head", "fsdp")),
        P(("groups", "head", "fsdp"), None, None),
        P(("groups", "ctx", "fsdp"), None),
        P(("groups", "ctx", "fsdp"), None),
        P(("groups", "ctx", "fsdp"), None),
        P(("groups", "ctx", "fsdp"), None),
        P("ctx", "fsdp", "head"),
        P("ctx", "fsdp", "head"),
        P("ctx", "head", "fsdp"),
    )
    out_specs = (
        P(("groups", "ctx"), ("head", "fsdp")),
        P(("groups", "ctx"), ("head", "fsdp")),
        P(("groups", "ctx"), ("head", "fsdp")),
        P(("groups", "ctx"), ("head", "fsdp")),
        P(("groups", "ctx"), ("head", "fsdp")),
        P(("groups", "ctx"), ("head", "fsdp"), None, None),
        P(("groups", "ctx", "fsdp"), "head"),
        P(("groups", "ctx", "fsdp"), "head"),
    )
    return jax.shard_map(
        per_device, mesh=mesh, in_specs=in_specs, out_specs=out_specs, check_vma=False
    )
```

```python
import functools

import jax
import jax.numpy as jnp
from jax import lax
from jax.experimental import pallas as pl
from jax.experimental.pallas import tpu as pltpu
from jax.sharding import PartitionSpec as P

BF = jnp.bfloat16
F32 = jnp.float32
VMEM_BYTES = 62 * 1024 * 1024
WEIGHT_SLOTS = 3
HEADS_STEPS = (4, 2, 1)
SMALL_BYTES = 12 * 1024 * 1024


def dot(a, b):
    return lax.dot_general(
        a.astype(BF), b.astype(BF), (((1,), (0,)), ((), ())), preferred_element_type=F32
    )


def dot_t(a, b):
    return lax.dot_general(
        a.astype(BF), b.astype(BF), (((1,), (1,)), ((), ())), preferred_element_type=F32
    )


def tdot(a, b):
    return lax.dot_general(
        a.astype(BF), b.astype(BF), (((0,), (0,)), ((), ())), preferred_element_type=F32
    )


def halves(x, axis):
    high = x.astype(BF)
    return jnp.concatenate([high, (x - high.astype(F32)).astype(BF)], axis=axis)


def places(size, axis):
    return lax.broadcasted_iota(jnp.int32, (size, size), axis)


def column(matrix, at):
    lanes = lax.broadcasted_iota(jnp.int32, matrix.shape, 1)
    return jnp.sum(jnp.where(lanes == at, matrix, 0.0), axis=1, keepdims=True)


def to_column(row):
    size = row.shape[1]
    spread = jnp.broadcast_to(row, (size, size))
    return jnp.sum(jnp.where(places(size, 0) == places(size, 1), spread, 0.0), axis=1, keepdims=True)


def inverse_less_one(scores):
    size = scores[0].shape[0]
    rows, cols = places(size, 0), places(size, 1)
    eye = (rows == cols).astype(F32)
    span, off = 1, None
    while span < size:
        joins = (rows // (2 * span) == cols // (2 * span)) & (rows // span != cols // span)
        parts = [jnp.where(joins, a, 0.0).astype(BF) for a in scores]
        if off is None:
            off = [-p.astype(F32) for p in parts]
        else:
            full = [(o + eye).astype(BF) for o in off]
            half = [dot(p, f) for p, f in zip(parts, full)]
            off = [o - dot(f, h) for o, f, h in zip(off, full, half)]
        span *= 2
    return off


def maps_kernel(
    chunk,
    width,
    heads_step,
    first,
    given,
    query_ref,
    key_ref,
    value_ref,
    decay_ref,
    rate_ref,
    grad_ref,
    *refs,
):
    (
        transfer_ref,
        carried_ref,
        own_ref,
        cum_ref,
        query_l_ref,
        key_l_ref,
        back_ref,
        lower_ref,
        score_ref,
    ) = refs[given:]
    tokens = query_ref.shape[0]
    chunks = tokens // chunk
    rows, cols = places(chunk, 0), places(chunk, 1)
    tri = (rows >= cols).astype(BF)
    tri = jnp.concatenate([tri, tri], axis=1)
    units = [(h, i) for h in range(heads_step) for i in range(chunks)]
    first = first + pl.program_id(0) * heads_step
    rate_cols = jnp.transpose(rate_ref[...])
    rates = [column(rate_cols, first + h) for h in range(heads_step)]

    def part(ref, unit):
        h, i = unit
        return ref[i * chunk : (i + 1) * chunk, h * width : (h + 1) * width]

    def unit_rows(x):
        return x * lax.rsqrt(jnp.sum(x * x, axis=-1, keepdims=True) + 1e-06)

    cums = [dot(tri, halves(part(decay_ref, u), 0)) for u in units]
    queries = [unit_rows(part(query_ref, u)) for u in units]
    keys = [unit_rows(part(key_ref, u)) for u in units]
    values = [part(value_ref, u) for u in units]
    middles = [0.5 * c[chunk - 1 : chunk, :] for c in cums]
    lifts = [jnp.exp(c - m) for c, m in zip(cums, middles)]
    sinks = [jnp.exp(m - c) for c, m in zip(cums, middles)]
    key_l = [(k * e).astype(BF) for k, e in zip(keys, lifts)]
    query_l = [(q * e).astype(BF) for q, e in zip(queries, lifts)]
    back = [
        (k * e * rates[h][i * chunk : (i + 1) * chunk]).astype(BF)
        for k, e, (h, i) in zip(keys, sinks, units)
    ]
    both = [dot_t(jnp.concatenate([k, q], axis=0), b) for k, q, b in zip(key_l, query_l, back)]
    key_scores = [jnp.where(rows > cols, s[:chunk], 0.0) for s in both]
    scores = [jnp.where(rows >= cols, s[chunk:], 0.0).astype(BF) for s in both]
    lower = [o.astype(BF) for o in inverse_less_one(key_scores)]
    wide = [jnp.concatenate([k, v.astype(BF)], axis=1) for k, v in zip(key_l, values)]
    solved = [
        dot(o, w) + jnp.concatenate([k.astype(F32), v], axis=1)
        for o, w, k, v in zip(lower, wide, key_l, values)
    ]
    solved = [s.astype(BF) for s in solved]
    stepped = [tdot(b, s) for b, s in zip(back, solved)]
    reads = [q.astype(F32) - dot(p, s[:, :width]) for q, p, s in zip(query_l, scores, solved)]
    mids = [to_column(jnp.exp(m)) for m in middles]
    owns = [m * tdot(r, part(grad_ref, u)) for m, r, u in zip(mids, reads, units)]
    for n, u in enumerate(units):
        h, i = u
        span = slice(i * chunk, (i + 1) * chunk)
        lanes = slice(h * width, (h + 1) * width)
        cum_ref[span, lanes] = cums[n]
        query_l_ref[span, lanes] = query_l[n]
        key_l_ref[span, lanes] = key_l[n]
        back_ref[span, lanes] = back[n]
        lower_ref[h, span, :] = lower[n]
        score_ref[h, span, :] = scores[n]
    eye = (places(width, 0) == places(width, 1)).astype(F32)
    for h in range(heads_step):
        state = None
        for i in range(chunks):
            n = h * chunks + i
            mid, step = mids[n], stepped[n][:, :width]
            entering = jnp.concatenate([eye, jnp.zeros_like(eye)], axis=1) if i == 0 else state
            scaled = mid * entering
            moved = scaled - dot(step, scaled)
            carried = jnp.concatenate([jnp.zeros_like(eye), stepped[n][:, width:]], axis=1)
            state = mid * (moved + carried)
        transfer_ref[h] = state[:, :width].astype(BF)
        carried_ref[h] = state[:, width:].astype(BF)
        total = owns[h * chunks + chunks - 1]
        for i in range(chunks - 2, -1, -1):
            n = h * chunks + i
            scaled = mids[n] * total
            total = owns[n] + mids[n] * (scaled - tdot(stepped[n][:, :width], scaled))
        own_ref[h] = total.astype(BF)


def grads_kernel(
    chunk,
    width,
    heads_step,
    first,
    heads_done,
    arrivals,
    given,
    place_ref,
    query_ref,
    key_ref,
    value_ref,
    rate_ref,
    grad_ref,
    cum_ref,
    query_l_ref,
    key_l_ref,
    back_ref,
    lower_ref,
    score_ref,
    start_ref,
    end_ref,
    *refs,
):
    first_head = first
    arrived_refs, before_refs, refs = refs[:arrivals], refs[arrivals : arrivals + given], refs[arrivals + given :]
    (
        query_grad_ref,
        key_grad_ref,
        value_grad_ref,
        decay_grad_ref,
        state_grad_ref,
        rate_grad_ref,
        rate_s,
    ) = refs
    position, last = place_ref[0], len(arrived_refs)

    def arrived(own_ref, h, turn):
        state = own_ref[h]
        for r, ref in enumerate(arrived_refs):
            state = jnp.where(position == turn(r + 1), ref[h].astype(F32), state)
        return state

    tokens = query_ref.shape[0]
    chunks = tokens // chunk
    rows, cols = places(chunk, 0), places(chunk, 1)
    tri = (rows <= cols).astype(BF)
    tri = jnp.concatenate([tri, tri], axis=1)
    first = first_head + pl.program_id(0) * heads_step
    heads = range(heads_step)
    rate_cols = jnp.transpose(rate_ref[...])
    rates = [column(rate_cols, first + h) for h in heads]

    def part(ref, h, i):
        return ref[i * chunk : (i + 1) * chunk, h * width : (h + 1) * width]

    def mat(ref, h, i):
        return ref[h, i * chunk : (i + 1) * chunk, :]

    cums = {(h, i): part(cum_ref, h, i) for i in range(chunks) for h in heads}
    middles = {u: 0.5 * c[chunk - 1 : chunk, :] for u, c in cums.items()}
    mids = {u: to_column(jnp.exp(m)) for u, m in middles.items()}
    states = {(h, 0): arrived(start_ref, h, lambda r: r) for h in heads}
    scaled, updates = {}, {}
    for i in range(chunks):
        for h in heads:
            u = (h, i)
            scaled[u] = mids[u] * states[u]
        rests = [part(value_ref, h, i) - dot(part(key_l_ref, h, i), scaled[h, i]) for h in heads]
        for h in heads:
            updates[h, i] = (rests[h] + dot(mat(lower_ref, h, i), rests[h])).astype(BF)
        for h in heads:
            moved = scaled[h, i] + tdot(part(back_ref, h, i), updates[h, i])
            states[h, i + 1] = mids[h, i] * moved
    out = {(h, chunks): arrived(end_ref, h, lambda r: last - r) for h in heads}
    rest_grads, lifted, out_grads = {}, {}, {}
    for i in range(chunks - 1, -1, -1):
        update_grads = []
        for h in heads:
            lifted[h, i] = mids[h, i] * out[h, i + 1]
            out_grads[h, i] = part(grad_ref, h, i).astype(BF)
            got = tdot(mat(score_ref, h, i), out_grads[h, i])
            update_grads.append(got + dot(part(back_ref, h, i), lifted[h, i]))
        for h in heads:
            rest = update_grads[h] + tdot(mat(lower_ref, h, i), update_grads[h])
            value_grad_ref[i * chunk : (i + 1) * chunk, h * width : (h + 1) * width] = rest
            rest_grads[h, i] = rest.astype(BF)
        for h in heads:
            left = jnp.concatenate([part(query_l_ref, h, i), part(key_l_ref, h, i)], axis=0)
            right = jnp.concatenate([out_grads[h, i], -rest_grads[h, i]], axis=0)
            out[h, i] = mids[h, i] * (lifted[h, i] + tdot(left, right))
    for h in heads:
        state_grad_ref[h] = out[h, 0]
    units = [(h, i) for i in range(chunks) for h in heads]
    joint = [jnp.concatenate([-rest_grads[u], out_grads[u]], axis=0) for u in units]
    pairs = [dot_t(j, updates[u]) for j, u in zip(joint, units)]
    key_pairs = [jnp.where(rows > cols, p[:chunk], 0.0).astype(BF) for p in pairs]
    query_pairs = [jnp.where(rows >= cols, p[chunk:], 0.0).astype(BF) for p in pairs]
    pairs = [jnp.concatenate([k, q], axis=0) for k, q in zip(key_pairs, query_pairs)]
    left_grads = [
        dot(p, part(back_ref, *u)) + dot_t(j, scaled[u]) for p, j, u in zip(pairs, joint, units)
    ]
    back_grads = [
        tdot(p, jnp.concatenate([part(key_l_ref, *u), part(query_l_ref, *u)], axis=0))
        + dot_t(updates[u], lifted[u])
        for p, u in zip(pairs, units)
    ]
    ones = jnp.ones((8, 2 * width), BF)
    crossing = [
        dot_t(ones, halves(out[h, i + 1] * states[h, i + 1], 1))[:1] for h, i in units
    ]
    slopes = [
        part(key_l_ref, *u).astype(F32) * l[:chunk]
        + part(query_l_ref, *u).astype(F32) * l[chunk:]
        - part(back_ref, *u).astype(F32) * b
        for u, l, b in zip(units, left_grads, back_grads)
    ]
    decays = [dot(tri, halves(s, 0)) + c for s, c in zip(slopes, crossing)]
    lanes = lax.broadcasted_iota(jnp.int32, (chunk, rate_s.shape[1]), 1)
    for n, (h, i) in enumerate(units):
        span = slice(i * chunk, (i + 1) * chunk)
        at = slice(h * width, (h + 1) * width)
        decay_grad_ref[span, at] = decays[n]
        gap = cums[h, i] - middles[h, i]
        lift, sink = jnp.exp(gap), jnp.exp(-gap)
        rate = rates[h][span]
        query, key = query_ref[span, at], key_ref[span, at]
        query_norm = lax.rsqrt(jnp.sum(query * query, axis=-1, keepdims=True) + 1e-06)
        key_norm = lax.rsqrt(jnp.sum(key * key, axis=-1, keepdims=True) + 1e-06)
        query, key = query * query_norm, key * key_norm
        query_grad = left_grads[n][chunk:] * lift
        sunk = back_grads[n] * sink
        key_grad = left_grads[n][:chunk] * lift + rate * sunk
        rate_grad = jnp.sum(sunk * key, axis=-1, keepdims=True)
        query_grad_ref[span, at] = query_norm * (
            query_grad - query * jnp.sum(query * query_grad, axis=-1, keepdims=True)
        )
        key_grad_ref[span, at] = key_norm * (
            key_grad - key * jnp.sum(key * key_grad, axis=-1, keepdims=True)
        )
        rate_s[span, :] = jnp.where(lanes == first + h, rate_grad, rate_s[span, :])

    @pl.when(pl.program_id(0) == pl.num_programs(0) - 1)
    def finish():
        rates_now = jnp.transpose(rate_s[...])[: rate_grad_ref.shape[0]]
        if given:
            rows_at = lax.broadcasted_iota(jnp.int32, rates_now.shape, 0)
            fresh = (rows_at >= first_head) & (rows_at < first_head + heads_done)
            rates_now = jnp.where(fresh, rates_now, before_refs[-1][...])
        rate_grad_ref[...] = rates_now


def heads_of_step(first, heads):
    return next(n for n in HEADS_STEPS if heads % n == 0 and first % n == 0)


def specs_of(tokens, width, chunk, heads_step, rate_heads, skip=0):
    lanes = pl.BlockSpec((tokens, heads_step * width), lambda h, *p: (0, skip + h))
    rate = pl.BlockSpec((rate_heads, tokens), lambda h, *p: (0, 0))
    square = pl.BlockSpec((heads_step, tokens, chunk), lambda h, *p: (skip + h, 0, 0))
    state = pl.BlockSpec((heads_step, width, width), lambda h, *p: (skip + h, 0, 0))
    return lanes, rate, square, state


def section_maps(
    queries, key_input, value_input, log_decay, write_rate, out_grad, first, heads, into=()
):
    heads_all, tokens = write_rate.shape
    width = queries.shape[1] // heads_all
    chunk = min(128, tokens)
    heads_step = heads_of_step(first, heads)
    lanes, rate, square, state = specs_of(
        tokens, width, chunk, heads_step, heads_all, first // heads_step
    )
    shape = jax.ShapeDtypeStruct
    return pl.pallas_call(
        functools.partial(maps_kernel, chunk, width, heads_step, first, len(into)),
        grid=(heads // heads_step,),
        in_specs=[lanes, lanes, lanes, lanes, rate, lanes]
        + [pl.BlockSpec(memory_space=pl.ANY)] * len(into),
        out_specs=[state, state, state, lanes, lanes, lanes, lanes, square, square],
        out_shape=[shape((heads_all, width, width), BF)] * 3
        + [shape(queries.shape, F32)]
        + [shape(queries.shape, BF)] * 3
        + [shape((heads_all, tokens, chunk), BF)] * 2,
        input_output_aliases={6 + n: n for n in range(len(into))},
        compiler_params=pltpu.CompilerParams(vmem_limit_bytes=VMEM_BYTES),
        cost_estimate=pl.CostEstimate(flops=10**8, bytes_accessed=10**7, transcendentals=0),
        name="section_maps",
    )(queries, key_input, value_input, log_decay, write_rate, out_grad, *into)


def section_grads(
    place,
    queries,
    key_input,
    value_input,
    write_rate,
    out_grad,
    saved,
    ends,
    arrivals,
    first,
    heads,
    into=(),
):
    heads_all, tokens = write_rate.shape
    width = queries.shape[1] // heads_all
    chunk = min(128, tokens)
    heads_step = heads_of_step(first, heads)
    lanes, rate, square, state = specs_of(
        tokens, width, chunk, heads_step, heads_all, first // heads_step
    )
    shape = jax.ShapeDtypeStruct
    args = (queries, key_input, value_input, write_rate, out_grad, *saved, *ends, *arrivals)
    kept = [pl.BlockSpec(memory_space=pl.ANY)] * 5 + [rate]
    return pl.pallas_call(
        functools.partial(
            grads_kernel, chunk, width, heads_step, first, heads, len(arrivals), len(into)
        ),
        grid_spec=pltpu.PrefetchScalarGridSpec(
            num_scalar_prefetch=1,
            grid=(heads // heads_step,),
            in_specs=[lanes, lanes, lanes, rate, lanes]
            + [lanes] * 4
            + [square] * 2
            + [state] * (2 + len(arrivals))
            + kept[: len(into)],
            out_specs=[lanes, lanes, lanes, lanes, state, rate],
            scratch_shapes=[pltpu.VMEM((tokens, 128), F32)],
        ),
        out_shape=[shape(queries.shape, F32)] * 4
        + [shape((heads_all, width, width), F32), shape((heads_all, tokens), F32)],
        input_output_aliases={1 + len(args) + n: n for n in range(len(into[:5]))},
        compiler_params=pltpu.CompilerParams(vmem_limit_bytes=VMEM_BYTES),
        name="section_grads",
    )(place, *args, *into)


def hop_kernel(backward_at, place_ref, transfer_ref, carried_ref, own_ref, *refs):
    heads = transfer_ref.shape[0]
    forward_state, backward_state, out_ref = refs[0], refs[-2], refs[-1]

    @pl.when(place_ref[0] == backward_at)
    def backward():
        for h in range(heads):
            out_ref[h] = (tdot(transfer_ref[h], backward_state[h]) + own_ref[h]).astype(BF)

    @pl.when(place_ref[0] != backward_at)
    def forward():
        for h in range(heads):
            out_ref[h] = (dot(transfer_ref[h], forward_state[h]) + carried_ref[h]).astype(BF)


def hop(place, transfer, carried, own_grad, states, turn, sections):
    spec = pl.BlockSpec(transfer.shape, lambda i, p: (0, 0, 0))
    leaving = pl.pallas_call(
        functools.partial(hop_kernel, sections - turn),
        grid_spec=pltpu.PrefetchScalarGridSpec(
            num_scalar_prefetch=1, grid=(1,), in_specs=[spec] * (3 + len(states)), out_specs=spec
        ),
        out_shape=jax.ShapeDtypeStruct(transfer.shape, BF),
        compiler_params=pltpu.CompilerParams(vmem_limit_bytes=SMALL_BYTES),
        name="hop",
    )(place, transfer, carried, own_grad, *states)
    pairs = [(turn - 1, turn), (sections - turn, sections - turn - 1)]
    return lax.ppermute(leaving, "ctx", pairs)


def experts_kernel(capacity, part_width, order, place_ref, *refs):
    sources = len(order)
    own_ref, came_refs, other_refs = refs[0], refs[1:sources], refs[sources : 2 * sources - 1]
    weight_refs, refs = refs[2 * sources - 1 : 2 * sources + 5], refs[2 * sources + 5 :]
    keep_ref, send_refs, scratch = refs[0], refs[1:3], refs[3:]
    weights_s, down_s, tokens_s, pieces_s, ranks_s, gates_s, sems = scratch
    step, steps = pl.program_id(0), pl.num_programs(0)
    mine, head_at, first, came_is = place_ref[0], place_ref[1], place_ref[2], place_ref[3]
    tokens = own_ref.shape[0]
    wide, hidden_width = down_s.shape[1:]
    padded = wide // 2
    experts = ranks_s.shape[1]
    many = tokens_s.shape[1]

    def weight_copies(expert, slot):
        for m in range(3):
            for far in range(2):
                part = mine if far == 0 else 1 - mine
                rows = pl.ds(pl.multiple_of(part * padded, 128), part_width)
                lanes = slice(m * hidden_width, (m + 1) * hidden_width)
                yield pltpu.make_async_copy(
                    weight_refs[2 * m + far].at[expert],
                    weights_s.at[slot, rows, lanes] if m < 2 else down_s.at[slot, rows],
                    sems.at[slot, 2 * m + far],
                )

    def choice(source, at):
        rank = ranks_s[source, pl.ds(at, 1), :]
        slot = lax.broadcasted_iota(jnp.int32, (capacity, tokens), 0).astype(F32)
        return slot == rank

    def choices(source):
        picks = [choice(source, first + e).astype(F32).astype(BF) for e in range(many)]
        return jnp.concatenate(picks, axis=0)

    slots = weights_s.shape[0]
    slot = lax.rem(step, slots)

    @pl.when(step == 0)
    def dispatch():
        for e in range(slots - 1):
            for copy in weight_copies(e, e):
                copy.start()
        for n in range(slots):
            for ref in (weights_s, down_s):
                blank = jnp.zeros((padded - part_width, ref.shape[2]), BF)
                ref[n, part_width:padded] = blank
                ref[n, padded + part_width :] = blank
        before = (places(tokens, 0) < places(tokens, 1)).astype(BF)
        for s, turn in enumerate(order):
            if turn == 0:
                came, other, kind = own_ref.at[:, :wide], own_ref.at[:, wide:], 0
            else:
                came, other, kind = came_refs[turn - 1], other_refs[turn - 1], came_is
            start = part_width // 128 * 128
            offset = part_width - start
            dense = jnp.transpose(came[:, start : start + 128].astype(F32))
            dense = dense[offset : offset + experts]
            named = dense > 0.0
            rank = dot(named.astype(F32), before)
            ranks_s[s] = jnp.where(named, rank, -1.0)
            gates_s[s] = dense
            pick = choices(s)
            for which, ref in ((kind, came), (1 - kind, other)):
                picked = dot(pick, ref[...]).astype(BF)
                for e in range(many):
                    span = slice(s * capacity, (s + 1) * capacity)
                    tokens_s[which, e, span] = picked[e * capacity : (e + 1) * capacity]

    @pl.when(step + slots - 1 < steps)
    def prefetch():
        for copy in weight_copies(step + slots - 1, lax.rem(step + slots - 1, slots)):
            copy.start()

    for copy in weight_copies(step, slot):
        copy.wait()
    at = first + step
    weight = jnp.concatenate(
        [
            jnp.sum(
                jnp.where(choice(s, at), gates_s[s, pl.ds(at, 1), :], 0.0), axis=1, keepdims=True
            )
            for s in range(sources)
        ],
        axis=0,
    )
    cut = hidden_width // (2 if hidden_width % 512 == 0 else 1)
    gate_part, gate_backs, up_backs = 0.0, [], []
    for f in range(0, hidden_width, cut):
        gate_pre = dot(tokens_s[0, step], weights_s[slot, :, f : f + cut])
        up_pre = dot(tokens_s[0, step], weights_s[slot, :, hidden_width + f : hidden_width + f + cut])
        raw_grad = dot(tokens_s[1, step], down_s[slot, :, f : f + cut])
        sigmoid = jax.nn.sigmoid(gate_pre)
        activated = gate_pre * sigmoid
        hidden = (activated * up_pre).astype(BF).astype(F32)
        gate_part = gate_part + jnp.sum(hidden * raw_grad, axis=1, keepdims=True)
        scaled = raw_grad * weight
        slope = sigmoid + activated * (1.0 - sigmoid)
        gate_backs.append((scaled * up_pre * slope).astype(BF))
        up_backs.append((scaled * activated).astype(BF))
    piece = dot_t(jnp.concatenate(gate_backs + up_backs, axis=1), weights_s[slot])
    lanes = lax.broadcasted_iota(jnp.int32, (1, wide), 1)
    here = (lanes == part_width + at) | (lanes == padded + part_width + at)
    piece = (piece + jnp.where(here, gate_part, 0.0)).astype(BF)
    for s in range(sources):
        pieces_s[s, step] = piece[s * capacity : (s + 1) * capacity]

    @pl.when(step == steps - 1)
    def combine():
        per = send_refs[0].shape[0]
        for s in range(sources):
            flat = pieces_s[s].reshape(many * capacity, wide)
            total = tdot(choices(s), flat).astype(BF)
            left, right = total[:, :padded], total[:, padded:]
            keep_ref[s] = jnp.where(head_at == 0, left, right)
            send_refs[s // per][s % per] = jnp.where(head_at == 0, right, left)


def expert_work(place, own, came, other, weights, capacity, total_experts, order):
    tokens, wide = came[0].shape
    many, part_width, hidden_width = weights[0].shape
    sources = len(order)
    padded = wide // 2
    slots = min(WEIGHT_SLOTS, many)
    whole = lambda x: pl.BlockSpec(x.shape, lambda e, p: (0,) * len(x.shape))
    shape = jax.ShapeDtypeStruct
    outs = [shape((n, tokens, padded), BF) for n in (sources, sources // 2, sources // 2)]
    token_args = (own, *came, *other)
    return pl.pallas_call(
        functools.partial(experts_kernel, capacity, part_width, order),
        grid_spec=pltpu.PrefetchScalarGridSpec(
            num_scalar_prefetch=1,
            grid=(many,),
            in_specs=[whole(x) for x in token_args]
            + [pl.BlockSpec(memory_space=pl.ANY)] * len(weights),
            out_specs=[whole(x) for x in outs],
            scratch_shapes=[
                pltpu.VMEM((slots, wide, 2 * hidden_width), BF),
                pltpu.VMEM((slots, wide, hidden_width), BF),
                pltpu.VMEM((2, many, sources * capacity, wide), BF),
                pltpu.VMEM((sources, many, capacity, wide), BF),
                pltpu.VMEM((sources, total_experts, tokens), F32),
                pltpu.VMEM((sources, total_experts, tokens), F32),
                pltpu.SemaphoreType.DMA((slots, 6)),
            ],
        ),
        out_shape=outs,
        compiler_params=pltpu.CompilerParams(vmem_limit_bytes=VMEM_BYTES),
        name="expert_work",
    )(place, *token_args, *weights)


def plain_call(kernel, name, out_shape, *args):
    return pl.pallas_call(
        kernel,
        out_shape=out_shape,
        compiler_params=pltpu.CompilerParams(vmem_limit_bytes=SMALL_BYTES),
        name=name,
    )(*args)


def head_sum_kernel(first, keep, got, *outs):
    for k, out in enumerate(outs):
        out[...] = (keep[first + k].astype(F32) + got[k].astype(F32)).astype(BF)


def home_kernel(part_width, experts, at_ref, ids_ref, *refs):
    pieces, (input_ref, gate_ref) = refs[:-2], refs[-2:]
    total = pieces[0][...].astype(F32)
    for piece in pieces[1:]:
        total = total + piece[...].astype(F32)
    total = jnp.transpose(total)
    input_ref[...] = total[:part_width]
    gates = total[part_width : part_width + experts]
    slots = gate_ref.shape[0]
    names = lax.broadcasted_iota(jnp.int32, gates.shape, 0)
    for j in range(slots):
        ids = ids_ref[pl.ds(at_ref[0] * slots + j, 1), :]
        gate_ref[j : j + 1, :] = jnp.sum(jnp.where(names == ids, gates, 0.0), axis=0, keepdims=True)


def swapped(x, axis):
    return lax.ppermute(x, axis, [(0, 1), (1, 0)])


def turned(x, axis, by):
    count = lax.axis_size(axis)
    return lax.ppermute(x, axis, [(i, (i + by) % count) for i in range(count)])


def pack_kernel(
    part_width, padded, which_ref, rows_ref, grads_ref, ids_ref, gates_ref, own_ref, sent_ref
):
    top, tokens = ids_ref.shape
    start = part_width // 128 * 128
    experts = lax.broadcasted_iota(jnp.int32, (128, tokens), 0) + (start - part_width)
    dense = jnp.zeros((128, tokens), F32)
    for j in range(top):
        named = experts == ids_ref[j : j + 1, :]
        dense = dense + jnp.where(named, gates_ref[j : j + 1, :], 0.0)
    dense = jnp.transpose(dense)
    lanes = lax.broadcasted_iota(jnp.int32, (tokens, 128), 1) + start
    wide = 2 * padded
    for n, ref in enumerate((rows_ref, grads_ref)):
        x = ref[...].astype(F32)
        x = jnp.concatenate([x, jnp.zeros((tokens, wide - x.shape[1]), F32)], axis=1)
        moved = pltpu.roll(x, padded - part_width, 1)
        tile = jnp.where(lanes < part_width, x[:, start : start + 128], dense)
        blank = jnp.zeros((tokens, padded - start - 128), F32)
        pieces = [x[:, :start], tile] + [blank] * (start + 128 < padded) + [moved[:, padded:]]
        packed = jnp.concatenate(pieces, axis=1).astype(BF)
        own_ref[:, n * wide : (n + 1) * wide] = packed

        @pl.when(which_ref[0] == n)
        def keep(packed=packed):
            sent_ref[...] = packed


def packed_tokens(first_is, rows, grads, ids, gates, part_width, padded):
    tokens = rows.shape[0]
    whole = lambda x: pl.BlockSpec(x.shape, lambda i, p: (0, 0))
    shapes = [jax.ShapeDtypeStruct((tokens, n * padded), BF) for n in (4, 2)]
    return pl.pallas_call(
        functools.partial(pack_kernel, part_width, padded),
        grid_spec=pltpu.PrefetchScalarGridSpec(
            num_scalar_prefetch=1,
            grid=(1,),
            in_specs=[whole(x) for x in (rows, grads, ids, gates)],
            out_specs=[whole(x) for x in shapes],
        ),
        out_shape=shapes,
        compiler_params=pltpu.CompilerParams(vmem_limit_bytes=VMEM_BYTES),
        name="packed_tokens",
    )(first_is, rows, grads, ids, gates)


def per_device(
    queries,
    key_input,
    value_input,
    log_decay,
    write_rate,
    start_state,
    out_grad,
    end_grad,
    moe_input,
    moe_grad,
    expert_ids,
    gate_weights,
    gate_matrix,
    up_matrix,
    down_matrix,
):
    sections = lax.axis_size("ctx")
    position = lax.axis_index("ctx")
    parts = lax.axis_size("fsdp")
    core = lax.axis_index("fsdp")
    head_count = lax.axis_size("head")
    head_at = lax.axis_index("head")

    token_count, top_count = expert_ids.shape
    experts_here = gate_matrix.shape[0]
    total_experts = experts_here * sections
    capacity = 3 * token_count // 8
    part_width = gate_matrix.shape[1]
    padded = -(-(part_width + total_experts) // 128) * 128

    turns = range(1, sections)
    near = [s for s in turns if s in (1, sections - 1)]
    far = [s for s in turns if s not in near]
    order = far + near + [0]
    came_is = head_at if head_count == 2 else 0 * head_at
    came_is = came_is.astype(jnp.int32)
    place = jnp.reshape(position, (1,)).astype(jnp.int32)
    recurrent = (queries, key_input, value_input, log_decay, write_rate.T, out_grad)
    heads_here = write_rate.shape[1]
    weights_own = [gate_matrix, up_matrix, jnp.swapaxes(down_matrix, 1, 2)]
    came, other, weights_far = {}, {}, [None] * 3

    def fetch_other(s):
        if head_count == 2:
            other[s] = swapped(came[s], "head")
        else:
            other[s] = turned(own[:, own.shape[1] // 2 :], "ctx", s)

    own, sent = packed_tokens(
        came_is.reshape(1), moe_input, moe_grad, expert_ids.T, gate_weights.T, part_width, padded
    )
    sent, recurrent, weights_own = lax.optimization_barrier((sent, recurrent, weights_own))
    for s in near:
        came[s] = turned(sent, "ctx", s)
    for m in range(2):
        weights_far[m] = swapped(weights_own[m], "fsdp")
    transfer, carried, own_grad, *saved = section_maps(*recurrent, 0, heads_here)
    came, weights_far[:2], transfer, sent, weights_own = lax.optimization_barrier(
        (came, weights_far[:2], transfer, sent, weights_own)
    )
    for s in far:
        came[s] = turned(sent, "ctx", s)
    for s in near:
        fetch_other(s)
    weights_far[2] = swapped(weights_own[2], "fsdp")
    maps = (transfer, carried, own_grad)
    arrivals = [hop(place, *maps, (start_state, end_grad), 1, sections)]
    came, other, arrivals = lax.optimization_barrier((came, other, arrivals))
    for s in far:
        fetch_other(s)
    if sections > 2:
        arrivals.append(hop(place, *maps, arrivals[-1:], 2, sections))
    other, arrivals = lax.optimization_barrier((other, arrivals))
    expert_place = jnp.stack([core, head_at, position * experts_here, came_is]).astype(jnp.int32)
    weights = [w for pair in zip(weights_own, weights_far) for w in pair]
    late = []
    for turn in range(3, sections):
        late.append(hop(place, *maps, (arrivals + late)[-1:], turn, sections))
    keep, *sends = expert_work(
        expert_place,
        own,
        [came[s] for s in turns],
        [other[s] for s in turns],
        weights,
        capacity,
        total_experts,
        order,
    )
    keep, sends, late = lax.optimization_barrier((keep, sends, late))
    arrivals = arrivals + late
    grad_args = (
        place,
        *(queries, key_input, value_input, write_rate.T, out_grad),
        saved,
        (start_state, end_grad),
        arrivals,
    )
    half = heads_here // 2
    rest = half + (heads_here - half) // 2
    gradients = section_grads(*grad_args, 0, half)
    if head_count == 2:
        others_sums = [swapped(send, "head") for send in sends]
        others_sums[0], gradients = lax.optimization_barrier((others_sums[0], gradients))
    if head_count == 2:
        shape = jax.ShapeDtypeStruct
        per = len(order) // 2
        block = (token_count, padded)
        pieces = []
        for n, (low, high) in enumerate(((half, rest), (rest, heads_here))):
            sums = plain_call(
                functools.partial(head_sum_kernel, n * per),
                "head_sum",
                [shape(block, BF)] * per,
                keep, others_sums[n],
            )
            sums, gradients, grad_args = lax.optimization_barrier((sums, gradients, grad_args))
            pieces += [
                turned(piece, "ctx", sections - turn) if turn else piece
                for turn, piece in zip(order[n * per : (n + 1) * per], sums)
            ]
            if high > low:
                gradients = section_grads(*grad_args, low, high - low, into=gradients)
            if n == 0:
                others_sums[1], gradients = lax.optimization_barrier((others_sums[1], gradients))
        pieces, gradients = lax.optimization_barrier((pieces, gradients))
        whole = lambda x: pl.BlockSpec(x.shape, lambda i, p: (0, 0))
        outs = [shape((part_width, token_count), F32), shape((top_count // 2, token_count), F32)]
        home_args = (expert_ids.T, *pieces)
        input_grads, gate_grads = pl.pallas_call(
            functools.partial(home_kernel, part_width, total_experts),
            grid_spec=pltpu.PrefetchScalarGridSpec(
                num_scalar_prefetch=1,
                grid=(1,),
                in_specs=[whole(x) for x in home_args],
                out_specs=[whole(x) for x in outs],
            ),
            out_shape=outs,
            compiler_params=pltpu.CompilerParams(vmem_limit_bytes=SMALL_BYTES),
            name="home",
        )(head_at.astype(jnp.int32).reshape(1), *home_args)
        input_grads, gate_grads = input_grads.T, gate_grads.T
    else:
        if heads_here > half:
            gradients = section_grads(*grad_args, half, heads_here - half, into=gradients)
        sent_back = jnp.concatenate(sends, axis=0)
        halves_in = [jnp.where(head_at == 0, keep, sent_back), jnp.where(head_at == 0, sent_back, keep)]
        wide = jnp.concatenate([x[:, :, :part_width] for x in halves_in], axis=-1)
        wide = lax.psum_scatter(wide, "head", scatter_dimension=2, tiled=True)
        gates = lax.psum(keep[:, :, part_width : part_width + total_experts], "head")
        pieces = jnp.concatenate([wide, gates], axis=-1)
        back = 0.0
        for piece, turn in zip(pieces, order):
            back = back + (turned(piece, "ctx", sections - turn) if turn else piece).astype(F32)
        input_grads, gates = back[:, : wide.shape[-1]], back[:, wide.shape[-1] :]
        slots_here = top_count // head_count
        ids_here = lax.dynamic_slice_in_dim(expert_ids, head_at * slots_here, slots_here, 1)
        named = ids_here[:, :, None] == lax.iota(jnp.int32, total_experts)[None, None, :]
        gate_grads = jnp.sum(jnp.where(named, gates[:, None, :], 0.0), axis=-1)
    return (*gradients[:4], gradients[5].T, gradients[4][None], input_grads, gate_grads)


def solution(mesh):
    in_specs = (
        P(("groups", "ctx"), ("head", "fsdp")),
        P(("groups", "ctx"), ("head", "fsdp")),
        P(("groups", "ctx"), ("head", "fsdp")),
        P(("groups", "ctx"), ("head", "fsdp")),
        P(("groups", "ctx"), ("head", "fsdp")),
        P(("groups", "head", "fsdp"), None, None),
        P(("groups", "ctx"), ("head", "fsdp")),
        P(("groups", "head", "fsdp"), None, None),
        P(("groups", "ctx", "fsdp"), None),
        P(("groups", "ctx", "fsdp"), None),
        P(("groups", "ctx", "fsdp"), None),
        P(("groups", "ctx", "fsdp"), None),
        P("ctx", "fsdp", "head"),
        P("ctx", "fsdp", "head"),
        P("ctx", "head", "fsdp"),
    )
    out_specs = (
        P(("groups", "ctx"), ("head", "fsdp")),
        P(("groups", "ctx"), ("head", "fsdp")),
        P(("groups", "ctx"), ("head", "fsdp")),
        P(("groups", "ctx"), ("head", "fsdp")),
        P(("groups", "ctx"), ("head", "fsdp")),
        P(("groups", "ctx"), ("head", "fsdp"), None, None),
        P(("groups", "ctx", "fsdp"), "head"),
        P(("groups", "ctx", "fsdp"), "head"),
    )
    return jax.shard_map(
        per_device, mesh=mesh, in_specs=in_specs, out_specs=out_specs, check_vma=False
    )
```

```python
import functools

import jax
import jax.numpy as jnp
from jax import lax
from jax.experimental import pallas as pl
from jax.experimental.pallas import tpu as pltpu
from jax.sharding import PartitionSpec as P

BF = jnp.bfloat16
F32 = jnp.float32
VMEM_BYTES = 62 * 1024 * 1024
WEIGHT_SLOTS = 3
HEADS_STEPS = (4, 2, 1)
SMALL_BYTES = 12 * 1024 * 1024


def dot(a, b):
    return lax.dot_general(
        a.astype(BF), b.astype(BF), (((1,), (0,)), ((), ())), preferred_element_type=F32
    )


def dot_t(a, b):
    return lax.dot_general(
        a.astype(BF), b.astype(BF), (((1,), (1,)), ((), ())), preferred_element_type=F32
    )


def tdot(a, b):
    return lax.dot_general(
        a.astype(BF), b.astype(BF), (((0,), (0,)), ((), ())), preferred_element_type=F32
    )


def halves(x, axis):
    high = x.astype(BF)
    return jnp.concatenate([high, (x - high.astype(F32)).astype(BF)], axis=axis)


def places(size, axis):
    return lax.broadcasted_iota(jnp.int32, (size, size), axis)


def column(matrix, at):
    lanes = lax.broadcasted_iota(jnp.int32, matrix.shape, 1)
    return jnp.sum(jnp.where(lanes == at, matrix, 0.0), axis=1, keepdims=True)


def to_column(row):
    size = row.shape[1]
    spread = jnp.broadcast_to(row, (size, size))
    return jnp.sum(jnp.where(places(size, 0) == places(size, 1), spread, 0.0), axis=1, keepdims=True)


def inverse_less_one(scores):
    size = scores[0].shape[0]
    rows, cols = places(size, 0), places(size, 1)
    eye = (rows == cols).astype(F32)
    span, off = 1, None
    while span < size:
        joins = (rows // (2 * span) == cols // (2 * span)) & (rows // span != cols // span)
        parts = [jnp.where(joins, a, 0.0).astype(BF) for a in scores]
        if off is None:
            off = [-p.astype(F32) for p in parts]
        else:
            full = [(o + eye).astype(BF) for o in off]
            half = [dot(p, f) for p, f in zip(parts, full)]
            off = [o - dot(f, h) for o, f, h in zip(off, full, half)]
        span *= 2
    return off


def maps_kernel(
    chunk,
    width,
    heads_step,
    first,
    given,
    query_ref,
    key_ref,
    value_ref,
    decay_ref,
    rate_ref,
    grad_ref,
    *refs,
):
    (
        transfer_ref,
        carried_ref,
        own_ref,
        cum_ref,
        query_l_ref,
        key_l_ref,
        back_ref,
        lower_ref,
        score_ref,
    ) = refs[given:]
    tokens = query_ref.shape[0]
    chunks = tokens // chunk
    rows, cols = places(chunk, 0), places(chunk, 1)
    tri = (rows >= cols).astype(BF)
    tri = jnp.concatenate([tri, tri], axis=1)
    units = [(h, i) for h in range(heads_step) for i in range(chunks)]
    first = first + pl.program_id(0) * heads_step
    rate_cols = jnp.transpose(rate_ref[...])
    rates = [column(rate_cols, first + h) for h in range(heads_step)]

    def part(ref, unit):
        h, i = unit
        return ref[i * chunk : (i + 1) * chunk, h * width : (h + 1) * width]

    def unit_rows(x):
        return x * lax.rsqrt(jnp.sum(x * x, axis=-1, keepdims=True) + 1e-06)

    cums = [dot(tri, halves(part(decay_ref, u), 0)) for u in units]
    queries = [unit_rows(part(query_ref, u)) for u in units]
    keys = [unit_rows(part(key_ref, u)) for u in units]
    values = [part(value_ref, u) for u in units]
    middles = [0.5 * c[chunk - 1 : chunk, :] for c in cums]
    lifts = [jnp.exp(c - m) for c, m in zip(cums, middles)]
    sinks = [jnp.exp(m - c) for c, m in zip(cums, middles)]
    key_l = [(k * e).astype(BF) for k, e in zip(keys, lifts)]
    query_l = [(q * e).astype(BF) for q, e in zip(queries, lifts)]
    back = [
        (k * e * rates[h][i * chunk : (i + 1) * chunk]).astype(BF)
        for k, e, (h, i) in zip(keys, sinks, units)
    ]
    both = [dot_t(jnp.concatenate([k, q], axis=0), b) for k, q, b in zip(key_l, query_l, back)]
    key_scores = [jnp.where(rows > cols, s[:chunk], 0.0) for s in both]
    scores = [jnp.where(rows >= cols, s[chunk:], 0.0).astype(BF) for s in both]
    lower = [o.astype(BF) for o in inverse_less_one(key_scores)]
    wide = [jnp.concatenate([k, v.astype(BF)], axis=1) for k, v in zip(key_l, values)]
    solved = [
        dot(o, w) + jnp.concatenate([k.astype(F32), v], axis=1)
        for o, w, k, v in zip(lower, wide, key_l, values)
    ]
    solved = [s.astype(BF) for s in solved]
    stepped = [tdot(b, s) for b, s in zip(back, solved)]
    reads = [q.astype(F32) - dot(p, s[:, :width]) for q, p, s in zip(query_l, scores, solved)]
    mids = [to_column(jnp.exp(m)) for m in middles]
    owns = [m * tdot(r, part(grad_ref, u)) for m, r, u in zip(mids, reads, units)]
    for n, u in enumerate(units):
        h, i = u
        span = slice(i * chunk, (i + 1) * chunk)
        lanes = slice(h * width, (h + 1) * width)
        cum_ref[span, lanes] = cums[n]
        query_l_ref[span, lanes] = query_l[n]
        key_l_ref[span, lanes] = key_l[n]
        back_ref[span, lanes] = back[n]
        lower_ref[h, span, :] = lower[n]
        score_ref[h, span, :] = scores[n]
    eye = (places(width, 0) == places(width, 1)).astype(F32)
    for h in range(heads_step):
        state = None
        for i in range(chunks):
            n = h * chunks + i
            mid, step = mids[n], stepped[n][:, :width]
            entering = jnp.concatenate([eye, jnp.zeros_like(eye)], axis=1) if i == 0 else state
            scaled = mid * entering
            moved = scaled - dot(step, scaled)
            carried = jnp.concatenate([jnp.zeros_like(eye), stepped[n][:, width:]], axis=1)
            state = mid * (moved + carried)
        transfer_ref[h] = state[:, :width].astype(BF)
        carried_ref[h] = state[:, width:].astype(BF)
        total = owns[h * chunks + chunks - 1]
        for i in range(chunks - 2, -1, -1):
            n = h * chunks + i
            scaled = mids[n] * total
            total = owns[n] + mids[n] * (scaled - tdot(stepped[n][:, :width], scaled))
        own_ref[h] = total.astype(BF)


def grads_kernel(
    chunk,
    width,
    heads_step,
    first,
    heads_done,
    arrivals,
    given,
    place_ref,
    query_ref,
    key_ref,
    value_ref,
    rate_ref,
    grad_ref,
    cum_ref,
    query_l_ref,
    key_l_ref,
    back_ref,
    lower_ref,
    score_ref,
    start_ref,
    end_ref,
    *refs,
):
    first_head = first
    arrived_refs, before_refs, refs = refs[:arrivals], refs[arrivals : arrivals + given], refs[arrivals + given :]
    (
        query_grad_ref,
        key_grad_ref,
        value_grad_ref,
        decay_grad_ref,
        state_grad_ref,
        rate_grad_ref,
        rate_s,
    ) = refs
    position, last = place_ref[0], len(arrived_refs)

    def arrived(own_ref, h, turn):
        state = own_ref[h]
        for r, ref in enumerate(arrived_refs):
            state = jnp.where(position == turn(r + 1), ref[h].astype(F32), state)
        return state

    tokens = query_ref.shape[0]
    chunks = tokens // chunk
    rows, cols = places(chunk, 0), places(chunk, 1)
    tri = (rows <= cols).astype(BF)
    tri = jnp.concatenate([tri, tri], axis=1)
    first = first_head + pl.program_id(0) * heads_step
    heads = range(heads_step)
    rate_cols = jnp.transpose(rate_ref[...])
    rates = [column(rate_cols, first + h) for h in heads]

    def part(ref, h, i):
        return ref[i * chunk : (i + 1) * chunk, h * width : (h + 1) * width]

    def mat(ref, h, i):
        return ref[h, i * chunk : (i + 1) * chunk, :]

    cums = {(h, i): part(cum_ref, h, i) for i in range(chunks) for h in heads}
    middles = {u: 0.5 * c[chunk - 1 : chunk, :] for u, c in cums.items()}
    mids = {u: to_column(jnp.exp(m)) for u, m in middles.items()}
    states = {(h, 0): arrived(start_ref, h, lambda r: r) for h in heads}
    scaled, updates = {}, {}
    for i in range(chunks):
        for h in heads:
            u = (h, i)
            scaled[u] = mids[u] * states[u]
        rests = [part(value_ref, h, i) - dot(part(key_l_ref, h, i), scaled[h, i]) for h in heads]
        for h in heads:
            updates[h, i] = (rests[h] + dot(mat(lower_ref, h, i), rests[h])).astype(BF)
        for h in heads:
            moved = scaled[h, i] + tdot(part(back_ref, h, i), updates[h, i])
            states[h, i + 1] = mids[h, i] * moved
    out = {(h, chunks): arrived(end_ref, h, lambda r: last - r) for h in heads}
    rest_grads, lifted, out_grads = {}, {}, {}
    for i in range(chunks - 1, -1, -1):
        update_grads = []
        for h in heads:
            lifted[h, i] = mids[h, i] * out[h, i + 1]
            out_grads[h, i] = part(grad_ref, h, i).astype(BF)
            got = tdot(mat(score_ref, h, i), out_grads[h, i])
            update_grads.append(got + dot(part(back_ref, h, i), lifted[h, i]))
        for h in heads:
            rest = update_grads[h] + tdot(mat(lower_ref, h, i), update_grads[h])
            value_grad_ref[i * chunk : (i + 1) * chunk, h * width : (h + 1) * width] = rest
            rest_grads[h, i] = rest.astype(BF)
        for h in heads:
            left = jnp.concatenate([part(query_l_ref, h, i), part(key_l_ref, h, i)], axis=0)
            right = jnp.concatenate([out_grads[h, i], -rest_grads[h, i]], axis=0)
            out[h, i] = mids[h, i] * (lifted[h, i] + tdot(left, right))
    for h in heads:
        state_grad_ref[h] = out[h, 0]
    units = [(h, i) for i in range(chunks) for h in heads]
    joint = [jnp.concatenate([-rest_grads[u], out_grads[u]], axis=0) for u in units]
    pairs = [dot_t(j, updates[u]) for j, u in zip(joint, units)]
    key_pairs = [jnp.where(rows > cols, p[:chunk], 0.0).astype(BF) for p in pairs]
    query_pairs = [jnp.where(rows >= cols, p[chunk:], 0.0).astype(BF) for p in pairs]
    pairs = [jnp.concatenate([k, q], axis=0) for k, q in zip(key_pairs, query_pairs)]
    left_grads = [
        dot(p, part(back_ref, *u)) + dot_t(j, scaled[u]) for p, j, u in zip(pairs, joint, units)
    ]
    back_grads = [
        tdot(p, jnp.concatenate([part(key_l_ref, *u), part(query_l_ref, *u)], axis=0))
        + dot_t(updates[u], lifted[u])
        for p, u in zip(pairs, units)
    ]
    ones = jnp.ones((8, 2 * width), BF)
    crossing = [
        dot_t(ones, halves(out[h, i + 1] * states[h, i + 1], 1))[:1] for h, i in units
    ]
    slopes = [
        part(key_l_ref, *u).astype(F32) * l[:chunk]
        + part(query_l_ref, *u).astype(F32) * l[chunk:]
        - part(back_ref, *u).astype(F32) * b
        for u, l, b in zip(units, left_grads, back_grads)
    ]
    decays = [dot(tri, halves(s, 0)) + c for s, c in zip(slopes, crossing)]
    lanes = lax.broadcasted_iota(jnp.int32, (chunk, rate_s.shape[1]), 1)
    for n, (h, i) in enumerate(units):
        span = slice(i * chunk, (i + 1) * chunk)
        at = slice(h * width, (h + 1) * width)
        decay_grad_ref[span, at] = decays[n]
        gap = cums[h, i] - middles[h, i]
        lift, sink = jnp.exp(gap), jnp.exp(-gap)
        rate = rates[h][span]
        query, key = query_ref[span, at], key_ref[span, at]
        query_norm = lax.rsqrt(jnp.sum(query * query, axis=-1, keepdims=True) + 1e-06)
        key_norm = lax.rsqrt(jnp.sum(key * key, axis=-1, keepdims=True) + 1e-06)
        query, key = query * query_norm, key * key_norm
        query_grad = left_grads[n][chunk:] * lift
        sunk = back_grads[n] * sink
        key_grad = left_grads[n][:chunk] * lift + rate * sunk
        rate_grad = jnp.sum(sunk * key, axis=-1, keepdims=True)
        query_grad_ref[span, at] = query_norm * (
            query_grad - query * jnp.sum(query * query_grad, axis=-1, keepdims=True)
        )
        key_grad_ref[span, at] = key_norm * (
            key_grad - key * jnp.sum(key * key_grad, axis=-1, keepdims=True)
        )
        rate_s[span, :] = jnp.where(lanes == first + h, rate_grad, rate_s[span, :])

    @pl.when(pl.program_id(0) == pl.num_programs(0) - 1)
    def finish():
        rates_now = jnp.transpose(rate_s[...])[: rate_grad_ref.shape[0]]
        if given:
            rows_at = lax.broadcasted_iota(jnp.int32, rates_now.shape, 0)
            fresh = (rows_at >= first_head) & (rows_at < first_head + heads_done)
            rates_now = jnp.where(fresh, rates_now, before_refs[-1][...])
        rate_grad_ref[...] = rates_now


def heads_of_step(first, heads):
    return next(n for n in HEADS_STEPS if heads % n == 0 and first % n == 0)


def specs_of(tokens, width, chunk, heads_step, rate_heads, skip=0):
    lanes = pl.BlockSpec((tokens, heads_step * width), lambda h, *p: (0, skip + h))
    rate = pl.BlockSpec((rate_heads, tokens), lambda h, *p: (0, 0))
    square = pl.BlockSpec((heads_step, tokens, chunk), lambda h, *p: (skip + h, 0, 0))
    state = pl.BlockSpec((heads_step, width, width), lambda h, *p: (skip + h, 0, 0))
    return lanes, rate, square, state


def section_maps(
    queries, key_input, value_input, log_decay, write_rate, out_grad, first, heads, into=()
):
    heads_all, tokens = write_rate.shape
    width = queries.shape[1] // heads_all
    chunk = min(128, tokens)
    heads_step = heads_of_step(first, heads)
    lanes, rate, square, state = specs_of(
        tokens, width, chunk, heads_step, heads_all, first // heads_step
    )
    shape = jax.ShapeDtypeStruct
    return pl.pallas_call(
        functools.partial(maps_kernel, chunk, width, heads_step, first, len(into)),
        grid=(heads // heads_step,),
        in_specs=[lanes, lanes, lanes, lanes, rate, lanes]
        + [pl.BlockSpec(memory_space=pl.ANY)] * len(into),
        out_specs=[state, state, state, lanes, lanes, lanes, lanes, square, square],
        out_shape=[shape((heads_all, width, width), BF)] * 3
        + [shape(queries.shape, F32)]
        + [shape(queries.shape, BF)] * 3
        + [shape((heads_all, tokens, chunk), BF)] * 2,
        input_output_aliases={6 + n: n for n in range(len(into))},
        compiler_params=pltpu.CompilerParams(vmem_limit_bytes=VMEM_BYTES),
        cost_estimate=pl.CostEstimate(flops=10**8, bytes_accessed=10**7, transcendentals=0),
        name="section_maps",
    )(queries, key_input, value_input, log_decay, write_rate, out_grad, *into)


def section_grads(
    place,
    queries,
    key_input,
    value_input,
    write_rate,
    out_grad,
    saved,
    ends,
    arrivals,
    first,
    heads,
    into=(),
):
    heads_all, tokens = write_rate.shape
    width = queries.shape[1] // heads_all
    chunk = min(128, tokens)
    heads_step = heads_of_step(first, heads)
    lanes, rate, square, state = specs_of(
        tokens, width, chunk, heads_step, heads_all, first // heads_step
    )
    shape = jax.ShapeDtypeStruct
    args = (queries, key_input, value_input, write_rate, out_grad, *saved, *ends, *arrivals)
    kept = [pl.BlockSpec(memory_space=pl.ANY)] * 5 + [rate]
    return pl.pallas_call(
        functools.partial(
            grads_kernel, chunk, width, heads_step, first, heads, len(arrivals), len(into)
        ),
        grid_spec=pltpu.PrefetchScalarGridSpec(
            num_scalar_prefetch=1,
            grid=(heads // heads_step,),
            in_specs=[lanes, lanes, lanes, rate, lanes]
            + [lanes] * 4
            + [square] * 2
            + [state] * (2 + len(arrivals))
            + kept[: len(into)],
            out_specs=[lanes, lanes, lanes, lanes, state, rate],
            scratch_shapes=[pltpu.VMEM((tokens, 128), F32)],
        ),
        out_shape=[shape(queries.shape, F32)] * 4
        + [shape((heads_all, width, width), F32), shape((heads_all, tokens), F32)],
        input_output_aliases={1 + len(args) + n: n for n in range(len(into[:5]))},
        compiler_params=pltpu.CompilerParams(vmem_limit_bytes=VMEM_BYTES),
        name="section_grads",
    )(place, *args, *into)


def hop_kernel(backward_at, place_ref, transfer_ref, carried_ref, own_ref, *refs):
    heads = transfer_ref.shape[0]
    forward_state, backward_state, out_ref = refs[0], refs[-2], refs[-1]

    @pl.when(place_ref[0] == backward_at)
    def backward():
        for h in range(heads):
            out_ref[h] = (tdot(transfer_ref[h], backward_state[h]) + own_ref[h]).astype(BF)

    @pl.when(place_ref[0] != backward_at)
    def forward():
        for h in range(heads):
            out_ref[h] = (dot(transfer_ref[h], forward_state[h]) + carried_ref[h]).astype(BF)


def hop(place, transfer, carried, own_grad, states, turn, sections):
    spec = pl.BlockSpec(transfer.shape, lambda i, p: (0, 0, 0))
    leaving = pl.pallas_call(
        functools.partial(hop_kernel, sections - turn),
        grid_spec=pltpu.PrefetchScalarGridSpec(
            num_scalar_prefetch=1, grid=(1,), in_specs=[spec] * (3 + len(states)), out_specs=spec
        ),
        out_shape=jax.ShapeDtypeStruct(transfer.shape, BF),
        compiler_params=pltpu.CompilerParams(vmem_limit_bytes=SMALL_BYTES),
        name="hop",
    )(place, transfer, carried, own_grad, *states)
    pairs = [(turn - 1, turn), (sections - turn, sections - turn - 1)]
    return lax.ppermute(leaving, "ctx", pairs)


def choice(ranks_s, source, at, capacity):
    rank = ranks_s[source, pl.ds(at, 1), :]
    slot = lax.broadcasted_iota(jnp.int32, (capacity, ranks_s.shape[2]), 0).astype(F32)
    return slot == rank


def choices(ranks_s, source, first, many, capacity):
    picks = [choice(ranks_s, source, first + e, capacity) for e in range(many)]
    return jnp.concatenate([pick.astype(F32).astype(BF) for pick in picks], axis=0)


def rank_tokens(tokens_ref, part_width, experts):
    tokens = tokens_ref.shape[0]
    start = part_width // 128 * 128
    dense = jnp.transpose(tokens_ref[:, start : start + 128].astype(F32))
    dense = dense[part_width - start : part_width - start + experts]
    named = dense > 0.0
    before = (places(tokens, 0) < places(tokens, 1)).astype(BF)
    return dense, jnp.where(named, dot(named.astype(F32), before), -1.0)


def dispatch_kernel(capacity, part_width, sources, place_ref, own_ref, *refs):
    came_refs, other_refs, out_ref, ranks_s = refs[: sources - 1], refs[sources - 1 : -2], refs[-2], refs[-1]
    first, came_is = place_ref[2], place_ref[3]
    many, wide = out_ref.shape[1], out_ref.shape[3]
    for s in range(sources):
        if s == sources - 1:
            came, other, kind = own_ref.at[:, :wide], own_ref.at[:, wide:], 0
        else:
            came, other, kind = came_refs[s], other_refs[s], came_is
        ranks_s[s] = rank_tokens(came, part_width, ranks_s.shape[1])[1]
        pick = choices(ranks_s, s, first, many, capacity)
        for which, ref in ((kind, came), (1 - kind, other)):
            picked = dot(pick, ref[...]).astype(BF)
            for e in range(many):
                span = slice(s * capacity, (s + 1) * capacity)
                out_ref[which, e, span] = picked[e * capacity : (e + 1) * capacity]


def dispatched(place, own, came, other, part_width, many, capacity, total_experts):
    tokens, wide = own.shape[0], own.shape[1] // 2
    sources = len(came) + 1
    whole = lambda x: pl.BlockSpec(x.shape, lambda i, p: (0,) * len(x.shape))
    out = jax.ShapeDtypeStruct((2, many, sources * capacity, wide), BF)
    args = (own, *came, *other)
    return pl.pallas_call(
        functools.partial(dispatch_kernel, capacity, part_width, sources),
        grid_spec=pltpu.PrefetchScalarGridSpec(
            num_scalar_prefetch=1,
            grid=(1,),
            in_specs=[whole(x) for x in args],
            out_specs=whole(out),
            scratch_shapes=[pltpu.VMEM((sources, total_experts, tokens), F32)],
        ),
        out_shape=out,
        compiler_params=pltpu.CompilerParams(vmem_limit_bytes=VMEM_BYTES),
        name="dispatched",
    )(place, *args)


def experts_kernel(capacity, part_width, order, late, place_ref, *refs):
    sources = len(order)
    own_ref, came_refs, other_refs = refs[0], refs[1:sources], refs[sources : sources + late]
    early_ref, refs = refs[sources + late], refs[sources + late + 1 :]
    weight_refs, refs = refs[:6], refs[6:]
    keep_ref, send_refs, scratch = refs[0], refs[1:3], refs[3:]
    weights_s, down_s, tokens_s, pieces_s, ranks_s, gates_s, sems = scratch
    step, steps = pl.program_id(0), pl.num_programs(0)
    mine, head_at, first, came_is = place_ref[0], place_ref[1], place_ref[2], place_ref[3]
    tokens = own_ref.shape[0]
    wide, hidden_width = down_s.shape[1:]
    padded = wide // 2
    experts = ranks_s.shape[1]
    many = tokens_s.shape[1]

    def weight_copies(expert, slot):
        for m in range(3):
            for far in range(2):
                part = mine if far == 0 else 1 - mine
                rows = pl.ds(pl.multiple_of(part * padded, 128), part_width)
                lanes = slice(m * hidden_width, (m + 1) * hidden_width)
                yield pltpu.make_async_copy(
                    weight_refs[2 * m + far].at[expert],
                    weights_s.at[slot, rows, lanes] if m < 2 else down_s.at[slot, rows],
                    sems.at[slot, 2 * m + far],
                )
        for which in range(2):
            yield pltpu.make_async_copy(
                early_ref.at[which, expert],
                tokens_s.at[which, expert, late * capacity :],
                sems.at[slot, 6 + which],
            )

    slots = weights_s.shape[0]
    slot = lax.rem(step, slots)

    @pl.when(step == 0)
    def dispatch():
        for e in range(slots - 1):
            for copy in weight_copies(e, e):
                copy.start()
        for n in range(slots):
            for ref in (weights_s, down_s):
                blank = jnp.zeros((padded - part_width, ref.shape[2]), BF)
                ref[n, part_width:padded] = blank
                ref[n, padded + part_width :] = blank
        for s, turn in enumerate(order):
            came = came_refs[turn - 1] if turn else own_ref
            gates_s[s], ranks_s[s] = rank_tokens(came, part_width, experts)
        for s, turn in enumerate(order[:late]):
            pick = choices(ranks_s, s, first, many, capacity)
            for which, ref in ((came_is, came_refs[turn - 1]), (1 - came_is, other_refs[s])):
                picked = dot(pick, ref[...]).astype(BF)
                for e in range(many):
                    span = slice(s * capacity, (s + 1) * capacity)
                    tokens_s[which, e, span] = picked[e * capacity : (e + 1) * capacity]

    @pl.when(step + slots - 1 < steps)
    def prefetch():
        for copy in weight_copies(step + slots - 1, lax.rem(step + slots - 1, slots)):
            copy.start()

    for copy in weight_copies(step, slot):
        copy.wait()
    at = first + step
    weight = jnp.concatenate(
        [
            jnp.sum(
                jnp.where(choice(ranks_s, s, at, capacity), gates_s[s, pl.ds(at, 1), :], 0.0), axis=1, keepdims=True
            )
            for s in range(sources)
        ],
        axis=0,
    )
    cut = hidden_width // (2 if hidden_width % 512 == 0 else 1)
    gate_part, gate_backs, up_backs = 0.0, [], []
    for f in range(0, hidden_width, cut):
        gate_pre = dot(tokens_s[0, step], weights_s[slot, :, f : f + cut])
        up_pre = dot(tokens_s[0, step], weights_s[slot, :, hidden_width + f : hidden_width + f + cut])
        raw_grad = dot(tokens_s[1, step], down_s[slot, :, f : f + cut])
        sigmoid = jax.nn.sigmoid(gate_pre)
        activated = gate_pre * sigmoid
        hidden = (activated * up_pre).astype(BF).astype(F32)
        gate_part = gate_part + jnp.sum(hidden * raw_grad, axis=1, keepdims=True)
        scaled = raw_grad * weight
        slope = sigmoid + activated * (1.0 - sigmoid)
        gate_backs.append((scaled * up_pre * slope).astype(BF))
        up_backs.append((scaled * activated).astype(BF))
    piece = dot_t(jnp.concatenate(gate_backs + up_backs, axis=1), weights_s[slot])
    lanes = lax.broadcasted_iota(jnp.int32, (1, wide), 1)
    here = (lanes == part_width + at) | (lanes == padded + part_width + at)
    piece = (piece + jnp.where(here, gate_part, 0.0)).astype(BF)
    for s in range(sources):
        pieces_s[s, step] = piece[s * capacity : (s + 1) * capacity]

    @pl.when(step == steps - 1)
    def combine():
        per = send_refs[0].shape[0]
        for s in range(sources):
            flat = pieces_s[s].reshape(many * capacity, wide)
            total = tdot(choices(ranks_s, s, first, many, capacity), flat).astype(BF)
            left, right = total[:, :padded], total[:, padded:]
            keep_ref[s] = jnp.where(head_at == 0, left, right)
            send_refs[s // per][s % per] = jnp.where(head_at == 0, right, left)


def expert_work(place, own, came, other, early, weights, capacity, total_experts, order):
    tokens, wide = came[0].shape
    many, part_width, hidden_width = weights[0].shape
    sources = len(order)
    padded = wide // 2
    slots = min(WEIGHT_SLOTS, many)
    whole = lambda x: pl.BlockSpec(x.shape, lambda e, p: (0,) * len(x.shape))
    shape = jax.ShapeDtypeStruct
    outs = [shape((n, tokens, padded), BF) for n in (sources, sources // 2, sources // 2)]
    token_args = (own, *came, *other)
    return pl.pallas_call(
        functools.partial(experts_kernel, capacity, part_width, order, len(other)),
        grid_spec=pltpu.PrefetchScalarGridSpec(
            num_scalar_prefetch=1,
            grid=(many,),
            in_specs=[whole(x) for x in token_args]
            + [pl.BlockSpec(memory_space=pl.ANY)] * (1 + len(weights)),
            out_specs=[whole(x) for x in outs],
            scratch_shapes=[
                pltpu.VMEM((slots, wide, 2 * hidden_width), BF),
                pltpu.VMEM((slots, wide, hidden_width), BF),
                pltpu.VMEM((2, many, sources * capacity, wide), BF),
                pltpu.VMEM((sources, many, capacity, wide), BF),
                pltpu.VMEM((sources, total_experts, tokens), F32),
                pltpu.VMEM((sources, total_experts, tokens), F32),
                pltpu.SemaphoreType.DMA((slots, 8)),
            ],
        ),
        out_shape=outs,
        compiler_params=pltpu.CompilerParams(vmem_limit_bytes=VMEM_BYTES),
        name="expert_work",
    )(place, *token_args, early, *weights)


def plain_call(kernel, name, out_shape, *args):
    return pl.pallas_call(
        kernel,
        out_shape=out_shape,
        compiler_params=pltpu.CompilerParams(vmem_limit_bytes=SMALL_BYTES),
        name=name,
    )(*args)


def head_sum_kernel(first, keep, got, *outs):
    for k, out in enumerate(outs):
        out[...] = (keep[first + k].astype(F32) + got[k].astype(F32)).astype(BF)


def home_kernel(part_width, experts, at_ref, ids_ref, *refs):
    pieces, (input_ref, gate_ref) = refs[:-2], refs[-2:]
    total = pieces[0][...].astype(F32)
    for piece in pieces[1:]:
        total = total + piece[...].astype(F32)
    total = jnp.transpose(total)
    input_ref[...] = total[:part_width]
    gates = total[part_width : part_width + experts]
    slots = gate_ref.shape[0]
    names = lax.broadcasted_iota(jnp.int32, gates.shape, 0)
    for j in range(slots):
        ids = ids_ref[pl.ds(at_ref[0] * slots + j, 1), :]
        gate_ref[j : j + 1, :] = jnp.sum(jnp.where(names == ids, gates, 0.0), axis=0, keepdims=True)


def swapped(x, axis):
    return lax.ppermute(x, axis, [(0, 1), (1, 0)])


def turned(x, axis, by):
    count = lax.axis_size(axis)
    return lax.ppermute(x, axis, [(i, (i + by) % count) for i in range(count)])


def pack_kernel(
    part_width, padded, which_ref, rows_ref, grads_ref, ids_ref, gates_ref, own_ref, sent_ref
):
    top, tokens = ids_ref.shape
    start = part_width // 128 * 128
    experts = lax.broadcasted_iota(jnp.int32, (128, tokens), 0) + (start - part_width)
    dense = jnp.zeros((128, tokens), F32)
    for j in range(top):
        named = experts == ids_ref[j : j + 1, :]
        dense = dense + jnp.where(named, gates_ref[j : j + 1, :], 0.0)
    dense = jnp.transpose(dense)
    lanes = lax.broadcasted_iota(jnp.int32, (tokens, 128), 1) + start
    wide = 2 * padded
    for n, ref in enumerate((rows_ref, grads_ref)):
        x = ref[...].astype(F32)
        x = jnp.concatenate([x, jnp.zeros((tokens, wide - x.shape[1]), F32)], axis=1)
        moved = pltpu.roll(x, padded - part_width, 1)
        tile = jnp.where(lanes < part_width, x[:, start : start + 128], dense)
        blank = jnp.zeros((tokens, padded - start - 128), F32)
        pieces = [x[:, :start], tile] + [blank] * (start + 128 < padded) + [moved[:, padded:]]
        packed = jnp.concatenate(pieces, axis=1).astype(BF)
        own_ref[:, n * wide : (n + 1) * wide] = packed

        @pl.when(which_ref[0] == n)
        def keep(packed=packed):
            sent_ref[...] = packed


def packed_tokens(first_is, rows, grads, ids, gates, part_width, padded):
    tokens = rows.shape[0]
    whole = lambda x: pl.BlockSpec(x.shape, lambda i, p: (0, 0))
    shapes = [jax.ShapeDtypeStruct((tokens, n * padded), BF) for n in (4, 2)]
    return pl.pallas_call(
        functools.partial(pack_kernel, part_width, padded),
        grid_spec=pltpu.PrefetchScalarGridSpec(
            num_scalar_prefetch=1,
            grid=(1,),
            in_specs=[whole(x) for x in (rows, grads, ids, gates)],
            out_specs=[whole(x) for x in shapes],
        ),
        out_shape=shapes,
        compiler_params=pltpu.CompilerParams(vmem_limit_bytes=VMEM_BYTES),
        name="packed_tokens",
    )(first_is, rows, grads, ids, gates)


def per_device(
    queries,
    key_input,
    value_input,
    log_decay,
    write_rate,
    start_state,
    out_grad,
    end_grad,
    moe_input,
    moe_grad,
    expert_ids,
    gate_weights,
    gate_matrix,
    up_matrix,
    down_matrix,
):
    sections = lax.axis_size("ctx")
    position = lax.axis_index("ctx")
    parts = lax.axis_size("fsdp")
    core = lax.axis_index("fsdp")
    head_count = lax.axis_size("head")
    head_at = lax.axis_index("head")

    token_count, top_count = expert_ids.shape
    experts_here = gate_matrix.shape[0]
    total_experts = experts_here * sections
    capacity = 3 * token_count // 8
    part_width = gate_matrix.shape[1]
    padded = -(-(part_width + total_experts) // 128) * 128

    turns = range(1, sections)
    near = [s for s in turns if s in (1, sections - 1)]
    far = [s for s in turns if s not in near]
    order = far + near + [0]
    came_is = head_at if head_count == 2 else 0 * head_at
    came_is = came_is.astype(jnp.int32)
    place = jnp.reshape(position, (1,)).astype(jnp.int32)
    recurrent = (queries, key_input, value_input, log_decay, write_rate.T, out_grad)
    heads_here = write_rate.shape[1]
    weights_own = [gate_matrix, up_matrix, jnp.swapaxes(down_matrix, 1, 2)]
    came, other, weights_far = {}, {}, [None] * 3

    def fetch_other(s):
        if head_count == 2:
            other[s] = swapped(came[s], "head")
        else:
            other[s] = turned(own[:, own.shape[1] // 2 :], "ctx", s)

    own, sent = packed_tokens(
        came_is.reshape(1), moe_input, moe_grad, expert_ids.T, gate_weights.T, part_width, padded
    )
    expert_place = jnp.stack([core, head_at, position * experts_here, came_is]).astype(jnp.int32)
    sent, recurrent, weights_own, expert_place = lax.optimization_barrier(
        (sent, recurrent, weights_own, expert_place)
    )
    for s in near:
        came[s] = turned(sent, "ctx", s)
    for m in range(2):
        weights_far[m] = swapped(weights_own[m], "fsdp")
    transfer, carried, own_grad, *saved = section_maps(*recurrent, 0, heads_here)
    came, weights_far[:2], transfer, sent, weights_own = lax.optimization_barrier(
        (came, weights_far[:2], transfer, sent, weights_own)
    )
    for s in far:
        came[s] = turned(sent, "ctx", s)
    for s in near:
        fetch_other(s)
    weights_far[2] = swapped(weights_own[2], "fsdp")
    maps = (transfer, carried, own_grad)
    arrivals = [hop(place, *maps, (start_state, end_grad), 1, sections)]
    came, other, arrivals = lax.optimization_barrier((came, other, arrivals))
    for s in far:
        fetch_other(s)
    if sections > 2:
        arrivals.append(hop(place, *maps, arrivals[-1:], 2, sections))
    early = dispatched(
        expert_place,
        own,
        [came[s] for s in near],
        [other[s] for s in near],
        part_width,
        experts_here,
        capacity,
        total_experts,
    )
    other, arrivals, early = lax.optimization_barrier((other, arrivals, early))
    weights = [w for pair in zip(weights_own, weights_far) for w in pair]
    late = []
    for turn in range(3, sections):
        late.append(hop(place, *maps, (arrivals + late)[-1:], turn, sections))
    keep, *sends = expert_work(
        expert_place,
        own,
        [came[s] for s in turns],
        [other[s] for s in far],
        early,
        weights,
        capacity,
        total_experts,
        order,
    )
    keep, sends, late = lax.optimization_barrier((keep, sends, late))
    arrivals = arrivals + late
    grad_args = (
        place,
        *(queries, key_input, value_input, write_rate.T, out_grad),
        saved,
        (start_state, end_grad),
        arrivals,
    )
    half = heads_here // 2
    rest = half + (heads_here - half) // 2
    gradients = section_grads(*grad_args, 0, half)
    if head_count == 2:
        others_sums = [swapped(send, "head") for send in sends]
        others_sums[0], gradients = lax.optimization_barrier((others_sums[0], gradients))
    if head_count == 2:
        shape = jax.ShapeDtypeStruct
        per = len(order) // 2
        block = (token_count, padded)
        pieces = []
        for n, (low, high) in enumerate(((half, rest), (rest, heads_here))):
            sums = plain_call(
                functools.partial(head_sum_kernel, n * per),
                "head_sum",
                [shape(block, BF)] * per,
                keep, others_sums[n],
            )
            sums, gradients, grad_args = lax.optimization_barrier((sums, gradients, grad_args))
            pieces += [
                turned(piece, "ctx", sections - turn) if turn else piece
                for turn, piece in zip(order[n * per : (n + 1) * per], sums)
            ]
            if high > low:
                gradients = section_grads(*grad_args, low, high - low, into=gradients)
            if n == 0:
                others_sums[1], gradients = lax.optimization_barrier((others_sums[1], gradients))
        pieces, gradients = lax.optimization_barrier((pieces, gradients))
        whole = lambda x: pl.BlockSpec(x.shape, lambda i, p: (0, 0))
        outs = [shape((part_width, token_count), F32), shape((top_count // 2, token_count), F32)]
        home_args = (expert_ids.T, *pieces)
        input_grads, gate_grads = pl.pallas_call(
            functools.partial(home_kernel, part_width, total_experts),
            grid_spec=pltpu.PrefetchScalarGridSpec(
                num_scalar_prefetch=1,
                grid=(1,),
                in_specs=[whole(x) for x in home_args],
                out_specs=[whole(x) for x in outs],
            ),
            out_shape=outs,
            compiler_params=pltpu.CompilerParams(vmem_limit_bytes=SMALL_BYTES),
            name="home",
        )(head_at.astype(jnp.int32).reshape(1), *home_args)
        input_grads, gate_grads = input_grads.T, gate_grads.T
    else:
        if heads_here > half:
            gradients = section_grads(*grad_args, half, heads_here - half, into=gradients)
        sent_back = jnp.concatenate(sends, axis=0)
        halves_in = [jnp.where(head_at == 0, keep, sent_back), jnp.where(head_at == 0, sent_back, keep)]
        wide = jnp.concatenate([x[:, :, :part_width] for x in halves_in], axis=-1)
        wide = lax.psum_scatter(wide, "head", scatter_dimension=2, tiled=True)
        gates = lax.psum(keep[:, :, part_width : part_width + total_experts], "head")
        pieces = jnp.concatenate([wide, gates], axis=-1)
        back = 0.0
        for piece, turn in zip(pieces, order):
            back = back + (turned(piece, "ctx", sections - turn) if turn else piece).astype(F32)
        input_grads, gates = back[:, : wide.shape[-1]], back[:, wide.shape[-1] :]
        slots_here = top_count // head_count
        ids_here = lax.dynamic_slice_in_dim(expert_ids, head_at * slots_here, slots_here, 1)
        named = ids_here[:, :, None] == lax.iota(jnp.int32, total_experts)[None, None, :]
        gate_grads = jnp.sum(jnp.where(named, gates[:, None, :], 0.0), axis=-1)
    return (*gradients[:4], gradients[5].T, gradients[4][None], input_grads, gate_grads)


def solution(mesh):
    in_specs = (
        P(("groups", "ctx"), ("head", "fsdp")),
        P(("groups", "ctx"), ("head", "fsdp")),
        P(("groups", "ctx"), ("head", "fsdp")),
        P(("groups", "ctx"), ("head", "fsdp")),
        P(("groups", "ctx"), ("head", "fsdp")),
        P(("groups", "head", "fsdp"), None, None),
        P(("groups", "ctx"), ("head", "fsdp")),
        P(("groups", "head", "fsdp"), None, None),
        P(("groups", "ctx", "fsdp"), None),
        P(("groups", "ctx", "fsdp"), None),
        P(("groups", "ctx", "fsdp"), None),
        P(("groups", "ctx", "fsdp"), None),
        P("ctx", "fsdp", "head"),
        P("ctx", "fsdp", "head"),
        P("ctx", "head", "fsdp"),
    )
    out_specs = (
        P(("groups", "ctx"), ("head", "fsdp")),
        P(("groups", "ctx"), ("head", "fsdp")),
        P(("groups", "ctx"), ("head", "fsdp")),
        P(("groups", "ctx"), ("head", "fsdp")),
        P(("groups", "ctx"), ("head", "fsdp")),
        P(("groups", "ctx"), ("head", "fsdp"), None, None),
        P(("groups", "ctx", "fsdp"), "head"),
        P(("groups", "ctx", "fsdp"), "head"),
    )
    return jax.shard_map(
        per_device, mesh=mesh, in_specs=in_specs, out_specs=out_specs, check_vma=False
    )
```
